32 devices in a mesh: dp: 16 (over z, y, x), head: 2 (over core).
Axes of the slice: x: 2, y: 2, z: 4, core: 2. Of those that a mesh axis runs over, the one named last changes fastest.
Arguments:
- token_ids: int32 [16384], P(('dp', 'head')), may hold values from 0 to 30719, as said below
- lengths: int32 [32], P(('dp', 'head')), may hold values from 64 to 512, as said below
- embed_table: bfloat16 [30720, 768], P('dp', 'head'), as said below
- qkv_weight: bfloat16 [3, 768, 768], P(None, None, 'head'), as said below
- out_weight: bfloat16 [768, 768], replicated, as said below
- first_gain: float32 [768], replicated, may hold values from 0.25 to 1.75
- first_bias: float32 [768], replicated, may hold values from -3 to 3
- in_weight: bfloat16 [768, 3072], replicated, may hold values from -0.21875 to 0.21875
- back_weight: bfloat16 [3072, 768], replicated, may hold values from -0.109375 to 0.109375
- second_gain: float32 [768], replicated, may hold values from 0.25 to 1.75
- term_vector: float32 [768], replicated, may hold values from -0.21875 to 0.21875
- cotangent: float32 [16384], P(('dp', 'head')), may hold values from -6 to 6
Outputs:
- term_weights: float32 [16384], P(('dp', 'head'))
- grad_table: float32 [30720, 768], P('dp', 'head')
- grad_qkv: float32 [3, 768, 768], P(None, 'dp', 'head')
- grad_out: float32 [768, 768], P(None, ('dp', 'head'))
- grad_in: float32 [768, 3072], P(None, ('dp', 'head'))
- grad_back: float32 [3072, 768], P(('dp', 'head'))
- grad_first_gain: float32 [768], P(('dp', 'head'))
- grad_first_bias: float32 [768], P(('dp', 'head'))
- grad_second_gain: float32 [768], P(('dp', 'head'))
- grad_term_vector: float32 [768], P(('dp', 'head'))
The draws below stay inside these ranges and needn't reach their ends.
Inputs may be any that keep to these rules, and one draw needn't show every extreme that they name: `token_ids`: in each aligned block of 1024 ids, at most 128 lie in any one range of 1920 rows that starts at a multiple of 1920, and some range holds exactly 128. `lengths`: some passage is full. `embed_table`: independent entries of deviation 1. `qkv_weight`: independent entries of deviation 1 / sqrt(768). `out_weight`: independent entries of deviation 1 / sqrt(6).
All inputs are finite; a program needn't handle non-finite values.
Results may differ from the reference program's by a relative error of at most 0.014.
Values may be sent and summed in bfloat16 or wider, within the bound.
No kernel may reach another device: no remote copies, remote signals or barrier semaphores. Data moves between devices by JAX's collectives and lax.ppermute only.
A program may use at most 128 MiB of HBM per device.

```python
import jax
import jax.numpy as jnp
from jax import lax

D = 768
HEADS = 12
HDIM = 64
FF = 3072
VOCAB = 30720
SEQ = 512
TOK_DEV = 512
TOKENS = 16384
PASSAGES = 32
OWNERS = 16
VROWS = 1920
CAP = 128


def bounded_normal(key, shape, deviation):
    return jax.random.truncated_normal(key, -6.0, 6.0, shape, jnp.float32) * deviation


def draw_embed_table(key, part):
    key = jax.random.fold_in(key, 11)
    return bounded_normal(key, (VOCAB, D), 1.0).astype(jnp.bfloat16)


def draw_qkv_weight(key, part):
    key = jax.random.fold_in(key, 12)
    deviation = 1.0 / D ** 0.5
    return bounded_normal(key, (3, D, D), deviation).astype(jnp.bfloat16)


def draw_out_weight(key, part):
    key = jax.random.fold_in(key, 13)
    deviation = 1.0 / max(1, D // 128) ** 0.5
    return bounded_normal(key, (D, D), deviation).astype(jnp.bfloat16)


def draw_token_ids(key, part):
    key = jax.random.fold_in(key, 14)
    block = 2 * TOK_DEV
    pair_count = TOKENS // block
    slot_count = OWNERS * CAP
    keys = jax.random.split(key, 5)
    scores = jax.random.randint(keys[0], (pair_count, slot_count), 0, 2 ** 14)
    hottest = jax.random.randint(keys[1], (pair_count, 1), 0, OWNERS)
    slot_owner = jnp.arange(slot_count, dtype=jnp.int32) // CAP
    scores = scores + jnp.where(slot_owner[None, :] == hottest, 2 ** 15, 0)
    scores = scores * slot_count + jnp.arange(slot_count, dtype=jnp.int32)[None, :]
    chosen = lax.top_k(scores, block)[1] // CAP
    order_score = jax.random.randint(keys[2], (pair_count, block), 0, 2 ** 14) * block + jnp.arange(block, dtype=jnp.int32)[None, :]
    order = jnp.argsort(order_score, axis=1)
    owner_rows = jnp.take_along_axis(chosen, order, axis=1)
    reach = jax.random.randint(keys[3], (pair_count, block), 1, VROWS + 1)
    within = jax.random.randint(keys[4], (pair_count, block), 0, reach)
    return (owner_rows * VROWS + within).reshape(TOKENS).astype(jnp.int32)


def draw_lengths(key, part):
    key = jax.random.fold_in(key, 15)
    keys = jax.random.split(key, 2)
    drawn = jax.random.randint(keys[0], (PASSAGES,), SEQ // 8, SEQ + 1)
    filled = jax.random.randint(keys[1], (), 0, PASSAGES)
    return jnp.where(jnp.arange(PASSAGES, dtype=jnp.int32) == filled, SEQ, drawn).astype(jnp.int32)


def block_scale(own_key, dims, cuts, smallest, high):
    def one(position, shards_of):
        steps = jax.random.uniform(jax.random.fold_in(jax.random.fold_in(own_key, 6), position), (shards_of,), jnp.float32, smallest / len(cuts), high / len(cuts))
        return jnp.repeat(jnp.exp(steps), dims[position] // shards_of).reshape((-1,) + (1,) * (len(dims) - position - 1))

    gain = one(*cuts[0])
    for cut in cuts[1:]:
        gain = gain * one(*cut)
    return gain


def centred(rng, shape, scale, limit, cuts=(), kind=jnp.bfloat16):
    loudness = block_scale(rng, shape, cuts, -0.22, 0.18) if cuts else 1.0
    array = jax.random.normal(rng, shape, jnp.float32) * scale * loudness
    return jnp.minimum(jnp.maximum(array, -limit), limit).astype(kind)


def setup_inputs(seed: int = 0) -> dict:
    arg_keys = jax.random.split(jax.random.key(seed), 13)
    return {
        "token_ids": draw_token_ids(jax.random.fold_in(arg_keys[12], 71), 0),
        "lengths": draw_lengths(jax.random.fold_in(arg_keys[12], 71), 0),
        "embed_table": draw_embed_table(jax.random.fold_in(arg_keys[12], 71), 0),
        "qkv_weight": draw_qkv_weight(jax.random.fold_in(arg_keys[12], 71), 0),
        "out_weight": draw_out_weight(jax.random.fold_in(arg_keys[12], 71), 0),
        "first_gain": jnp.clip(1.0 + 0.15 * jax.random.normal(arg_keys[5], (D,), jnp.float32), 0.25, 1.75),
        "first_bias": centred(arg_keys[6], (D,), 0.3, 3.0, (), jnp.float32),
        "in_weight": centred(arg_keys[7], (D, FF), D ** -0.5, 0.21875),
        "back_weight": centred(arg_keys[8], (FF, D), FF ** -0.5, 0.109375),
        "second_gain": jnp.clip(1.0 + 0.15 * jax.random.normal(arg_keys[9], (D,), jnp.float32), 0.25, 1.75),
        "term_vector": centred(arg_keys[10], (D,), D ** -0.5, 0.21875, (), jnp.float32),
        "cotangent": centred(arg_keys[11], (TOKENS,), 1.0, 6.0, ((0, 32),), jnp.float32),
    }


@jax.custom_vjp
def low(v):
    return lax.optimization_barrier(v.astype(jnp.bfloat16)).astype(jnp.float32)

@jax.custom_vjp
def low_back(v):
    return v

def low_keep(v):
    return (low(v), None)

def low_pass(kept, grad):
    return (grad,)

def back_keep(v):
    return (v, None)

def back_low(kept, grad):
    return (low(grad),)
low.defvjp(low_keep, low_pass)
low_back.defvjp(back_keep, back_low)

def layer_norm(values, norm_gain, norm_bias):
    centre = values - lax.optimization_barrier(jnp.mean(values, -1, keepdims=True))
    spread = lax.optimization_barrier(jnp.mean(centre * centre, -1, keepdims=True))
    return centre * lax.rsqrt(spread + 1e-12) * norm_gain + norm_bias

def gain_norm(values, norm_gain):
    centre = values - lax.optimization_barrier(jnp.mean(values, -1, keepdims=True))
    spread = lax.optimization_barrier(jnp.mean(centre * centre, -1, keepdims=True))
    return centre * lax.rsqrt(spread + 1e-12) * norm_gain

def attend(pieces):
    highest = lax.Precision.HIGHEST
    query_rows, key_rows, value_rows, length = pieces
    raw_scores = jnp.einsum('qhd,khd->hqk', query_rows, key_rows, precision=highest)
    scores = low_back(raw_scores * 0.125)
    key_live = jnp.arange(SEQ, dtype=jnp.int32) < length
    logits = jnp.where(key_live[None, None, :], scores, -1e+30)
    row_top = lax.optimization_barrier(jnp.max(logits, -1, keepdims=True))
    powers = jnp.exp(logits - row_top)
    attn_probs = low(powers / lax.optimization_barrier(jnp.sum(powers, -1, keepdims=True)))
    result = jnp.einsum('hqk,khd->qhd', attn_probs, value_rows, precision=highest)
    return low(low_back(result)).reshape(SEQ, HEADS * HDIM)

def forward(embed_table, qkv_weight, out_weight, first_gain, first_bias, in_weight, back_weight, second_gain, term_vector, id_block, length_block):
    highest = lax.Precision.HIGHEST
    seq_count = length_block.shape[0]
    block_rows = seq_count * SEQ
    head_shape = (seq_count, SEQ, HEADS, HDIM)
    embedded = jnp.take(embed_table, id_block, axis=0)
    queries = low(low_back(jnp.dot(embedded, qkv_weight[0], precision=highest))).reshape(head_shape)
    key_all = low(low_back(jnp.dot(embedded, qkv_weight[1], precision=highest))).reshape(head_shape)
    value_all = low(low_back(jnp.dot(embedded, qkv_weight[2], precision=highest))).reshape(head_shape)
    attended = lax.map(jax.checkpoint(attend), (queries, key_all, value_all, length_block)).reshape(block_rows, HEADS * HDIM)
    branch = low_back(jnp.dot(attended, out_weight, precision=highest))
    normed = layer_norm(embedded + branch, first_gain, first_bias)
    inner_pre = low_back(jnp.dot(low(normed), in_weight, precision=highest))
    active = low(jax.nn.gelu(inner_pre, approximate=False))
    outer_out = low_back(jnp.dot(active, back_weight, precision=highest))
    final_rows = gain_norm(normed + outer_out, second_gain)
    logit_rows = jnp.dot(final_rows, term_vector, precision=highest)
    positions = jnp.arange(block_rows, dtype=jnp.int32) % SEQ
    live_mask = (positions < jnp.repeat(length_block, SEQ)).astype(jnp.float32)
    return jax.nn.softplus(logit_rows) * live_mask

def reference(token_ids, lengths, embed_table, qkv_weight, out_weight, first_gain, first_bias, in_weight, back_weight, second_gain, term_vector, cotangent):
    group_size = 1
    for option in (2, 4, 8):
        if PASSAGES % option == 0:
            group_size = option
    group_count = PASSAGES // group_size
    group_rows = group_size * SEQ
    primal_args = (embed_table.astype(jnp.float32), qkv_weight.astype(jnp.float32), out_weight.astype(jnp.float32), first_gain, first_bias, in_weight.astype(jnp.float32), back_weight.astype(jnp.float32), second_gain, term_vector)
    id_groups = token_ids.reshape(group_count, group_rows)
    length_groups = lengths.reshape(group_count, group_size)
    cot_groups = cotangent.reshape(group_count, group_rows)

    def one_group(totals, pieces):
        id_block, length_block, cot_block = pieces

        def closed(table_a, qkv_a, out_a, gain_a, bias_a, in_a, back_a, gain_b, term_a):
            return forward(table_a, qkv_a, out_a, gain_a, bias_a, in_a, back_a, gain_b, term_a, id_block, length_block)
        outputs, pullback = jax.vjp(closed, *primal_args)
        grads = pullback(cot_block)
        return (tuple((total + grad for total, grad in zip(totals, grads))), outputs)
    zero_grads = tuple((jnp.zeros_like(item) for item in primal_args))
    totals, outputs = lax.scan(one_group, zero_grads, (id_groups, length_groups, cot_groups))
    term_weights = outputs.reshape(PASSAGES * SEQ)
    return (term_weights, totals[0], totals[1], totals[2], totals[5], totals[6], totals[3], totals[4], totals[7], totals[8])
```

```python
import functools

import jax
import jax.numpy as jnp
from jax import lax
from jax.experimental import pallas as pl
from jax.experimental.pallas import tpu as pltpu
from jax.sharding import PartitionSpec as P

HDIM = 64
LOG2E = 1.4426950408889634
BF = jnp.bfloat16
F32 = jnp.float32
VMEM_LIMIT = 48 * 1024 * 1024


def dot_nn(a, b):
    return lax.dot_general(a, b, (((1,), (0,)), ((), ())), preferred_element_type=F32)


def dot_nt(a, b):
    return lax.dot_general(a, b, (((1,), (1,)), ((), ())), preferred_element_type=F32)


def dot_tn(a, b):
    return lax.dot_general(a, b, (((0,), (0,)), ((), ())), preferred_element_type=F32)


def iota(shape, dim):
    return lax.broadcasted_iota(jnp.int32, shape, dim)


def params(**more):
    return pltpu.CompilerParams(vmem_limit_bytes=VMEM_LIMIT, **more)


def whole(shape):
    return pl.BlockSpec(shape, lambda *_: (0,) * len(shape))


def cost(flops, moved, trans=0):
    return pl.CostEstimate(flops=int(flops), bytes_accessed=int(moved), transcendentals=int(trans))


def pick_kernel(place, ids_ref, table_ref, picked_ref, asked_ref, row_ref, col_ref, rank_s, hi_s, lo_s, hot_s):
    owners, block = ids_ref.shape
    rows = table_ref.shape[0]
    cap = picked_ref.shape[0] // owners
    dp = place[0]
    ids = ids_ref[...]
    away = ids - dp * rows
    mine = (away >= 0) & (away < rows)
    floor = iota((owners, block), 0) * rows
    own_ids = ids_ref[0:1, :]
    marks = (own_ids >= floor) & (own_ids < floor + rows)
    both = jnp.concatenate([mine.astype(F32), marks.astype(F32)], axis=0).astype(BF)
    upto = (iota((block, block), 0) <= iota((block, block), 1)).astype(F32).astype(BF)
    counts = dot_nn(both, upto)
    rank_s[...] = jnp.where(mine, counts[:owners], 0.0) - 1.0
    hi_s[...] = (away >> 6).astype(F32)
    lo_s[...] = (away & 63).astype(F32)
    spot = jnp.where(marks, counts[owners:] - 1.0 + iota((owners, block), 0).astype(F32) * cap, 0.0)
    slot = jnp.sum(spot, axis=0, keepdims=True)
    row_ref[...] = jnp.broadcast_to(slot, row_ref.shape)
    col_ref[...] = jnp.transpose(jnp.broadcast_to(slot, (128, block)))
    group = hot_s.shape[0] // cap

    def per_group(g, _):
        def per_block(i, _):
            j = g * group + i
            r = j ^ dp
            rank = rank_s[pl.ds(r, 1), :].astype(jnp.int32)
            sel = (iota((cap, block), 0) == rank).astype(F32).astype(BF)
            lane = iota((16, block), 0)
            code = jnp.where(lane == 0, hi_s[pl.ds(r, 1), :], jnp.where(lane == 1, lo_s[pl.ds(r, 1), :], 0.0)).astype(BF)
            cols = dot_nt(sel, code)
            asked_col = (cols[:, 0:1] * 64.0 + cols[:, 1:2]).astype(jnp.int32)
            lines = dot_nt(code, sel)
            asked_ref[pl.ds(j, 1), :] = lines[0:1, :] * 64.0 + lines[1:2, :]
            hot = (iota((cap, rows), 1) == asked_col).astype(F32).astype(BF)
            hot_s[pl.ds(pl.multiple_of(i * cap, cap), cap), :] = hot
            return 0

        lax.fori_loop(0, group, per_block, 0)
        size = group * cap
        picked_ref[pl.ds(pl.multiple_of(g * size, size), size), :] = dot_nn(hot_s[...], table_ref[...]).astype(BF)
        return 0

    lax.fori_loop(0, owners // group, per_group, 0)


def pick(dp, ids, table, cap):
    owners, block = ids.shape
    rows, half = table.shape
    group = min(owners, max(1, 512 // cap))
    shapes = (
        jax.ShapeDtypeStruct((owners * cap, half), BF),
        jax.ShapeDtypeStruct((owners, cap), F32),
        jax.ShapeDtypeStruct((8, block), F32),
        jax.ShapeDtypeStruct((block, 128), F32),
    )
    return pl.pallas_call(
        pick_kernel,
        grid_spec=pltpu.PrefetchScalarGridSpec(
            num_scalar_prefetch=1,
            grid=(1,),
            in_specs=[whole(ids.shape), whole(table.shape)],
            out_specs=[whole(s.shape) for s in shapes],
            scratch_shapes=[pltpu.VMEM((owners, block), F32)] * 3 + [pltpu.VMEM((group * cap, rows), BF)],
        ),
        out_shape=shapes,
        compiler_params=params(),
        name="pick",
    )(dp, ids, table)


def regather_kernel(col_ref, got_ref, own_ref, send_ref):
    slots = got_ref.shape[0]
    half = own_ref.shape[0]
    for part, out in ((1, send_ref), (0, own_ref)):
        slot = col_ref[part * half : (part + 1) * half, 0:1].astype(jnp.int32)
        hot = (iota((half, slots), 1) == slot).astype(F32).astype(BF)
        out[...] = dot_nn(hot, got_ref[...]).astype(BF)


def regather(col, got):
    block, half = col.shape[0], got.shape[1]
    shapes = [jax.ShapeDtypeStruct((block // 2, half), BF)] * 2
    return pl.pallas_call(
        regather_kernel,
        grid=(1,),
        in_specs=[whole(col.shape), whole(got.shape)],
        out_specs=[whole(s.shape) for s in shapes],
        out_shape=shapes,
        compiler_params=params(),
        name="regather",
    )(col, got)


def spread_kernel(row_ref, own_ref, other_ref, out_ref):
    half = own_ref.shape[0]
    step = out_ref.shape[0]
    base = pl.program_id(0) * step
    slot = row_ref[0:1, :].astype(jnp.int32)
    place = iota((step, half), 0) + base
    hot_own = (place == slot[:, :half]).astype(F32).astype(BF)
    hot_other = (place == slot[:, half:]).astype(F32).astype(BF)
    out_ref[...] = (dot_nn(hot_own, own_ref[...]) + dot_nn(hot_other, other_ref[...])).astype(BF)


def spread(row, own, other, slots):
    step = 512
    return pl.pallas_call(
        spread_kernel,
        grid=(slots // step,),
        in_specs=[whole(row.shape), whole(own.shape), whole(other.shape)],
        out_specs=pl.BlockSpec((step, own.shape[1]), lambda i: (i, 0)),
        out_shape=jax.ShapeDtypeStruct((slots, own.shape[1]), BF),
        compiler_params=params(),
        name="spread",
    )(row, own, other)


def table_kernel(asked_ref, got_ref, out_ref):
    step = out_ref.shape[0]
    base = pl.program_id(0) * step
    total = jnp.zeros(out_ref.shape, F32)
    lines, width = asked_ref.shape
    for c in range(lines):
        asked = asked_ref[c : c + 1, :].astype(jnp.int32)
        hot = (iota((step, width), 0) + base == asked).astype(F32).astype(BF)
        total = total + dot_nn(hot, got_ref[c * width : (c + 1) * width, :])
    out_ref[...] = total


def table_grad(asked, got, rows):
    step = 640 if rows % 640 == 0 else rows
    return pl.pallas_call(
        table_kernel,
        grid=(rows // step,),
        in_specs=[whole(asked.shape), whole(got.shape)],
        out_specs=pl.BlockSpec((step, got.shape[1]), lambda i: (i, 0)),
        out_shape=jax.ShapeDtypeStruct((rows, got.shape[1]), F32),
        compiler_params=params(),
        name="table_grad",
    )(asked, got)


def attend_kernel(place, own_ref, other_ref, weight_ref, emb_ref, proj_ref, out_ref, stat_ref):
    half = own_ref.shape[1]
    length = place[1]

    @pl.when(pl.program_id(0) == 0)
    def _():
        @pl.when(place[0] == 0)
        def _():
            emb_ref[:, :half] = own_ref[...]
            emb_ref[:, half:] = other_ref[...]

        @pl.when(place[0] != 0)
        def _():
            emb_ref[:, :half] = other_ref[...]
            emb_ref[:, half:] = own_ref[...]

    emb = emb_ref[...]
    seq = emb.shape[0]
    query = dot_nn(emb, weight_ref[0]).astype(BF)
    key = dot_nn(emb, weight_ref[1]).astype(BF)
    value = dot_nn(emb, weight_ref[2]).astype(BF)
    proj_ref[0] = query
    proj_ref[1] = key
    proj_ref[2] = value
    lane = iota(query.shape, 1)
    live = iota((seq, seq), 0) < length
    value_t = jnp.transpose(value)
    parts = []
    for h in range(2):
        this = (lane < HDIM) if h == 0 else (lane >= HDIM)
        masked = jnp.where(this, query, jnp.zeros_like(query))
        score = jnp.where(live, dot_nt(key, masked) * (0.125 * LOG2E), -1e30)
        top = jnp.max(score, axis=0, keepdims=True)
        power = jnp.exp2(score - top)
        total = jnp.sum(power, axis=0, keepdims=True)
        share = 1.0 / total
        stat_ref[0, 2 * h : 2 * h + 1, :] = top
        stat_ref[0, 2 * h + 1 : 2 * h + 2, :] = share
        low = (power * share).astype(BF)
        parts.append(dot_nn(value_t, low))
    picked = jnp.where(iota(parts[0].shape, 0) < HDIM, parts[0], parts[1])
    out_ref[...] = jnp.transpose(picked).astype(BF)


def attend(place, own, other, weight):
    seq, half = own.shape
    width = 2 * half
    pairs = width // 128
    shapes = (
        jax.ShapeDtypeStruct((seq, width), BF),
        jax.ShapeDtypeStruct((3, seq, width), BF),
        jax.ShapeDtypeStruct((seq, width), BF),
        jax.ShapeDtypeStruct((pairs, 8, seq), F32),
    )
    return pl.pallas_call(
        attend_kernel,
        grid_spec=pltpu.PrefetchScalarGridSpec(
            num_scalar_prefetch=1,
            grid=(pairs,),
            in_specs=[
                whole(own.shape),
                whole(other.shape),
                pl.BlockSpec((3, width, 128), lambda i, s: (0, 0, i)),
            ],
            out_specs=[
                whole((seq, width)),
                pl.BlockSpec((3, seq, 128), lambda i, s: (0, 0, i)),
                pl.BlockSpec((seq, 128), lambda i, s: (0, i)),
                pl.BlockSpec((1, 8, seq), lambda i, s: (i, 0, 0)),
            ],
        ),
        out_shape=shapes,
        compiler_params=params(),
        name="attend",
    )(place, own, other, weight)


def attend_back_kernel(place, proj_ref, grad_ref, stat_ref, weight_ref, sum_ref, gproj_ref, own_ref, send_ref, total_s):
    step = pl.program_id(0)
    length = place[1]
    query, key, value = proj_ref[0], proj_ref[1], proj_ref[2]
    grad = grad_ref[...]
    seq = grad.shape[0]
    lane = iota(query.shape, 1)
    live = iota((seq, seq), 0) < length
    key_t = jnp.transpose(key)
    outs = []
    for h in range(2):
        this = (lane < HDIM) if h == 0 else (lane >= HDIM)
        masked = jnp.where(this, query, jnp.zeros_like(query))
        grad_h = jnp.where(this, grad, jnp.zeros_like(grad))
        score = jnp.where(live, dot_nt(key, masked) * (0.125 * LOG2E), -1e30)
        probs = jnp.exp2(score - stat_ref[0, 2 * h : 2 * h + 1, :]) * stat_ref[0, 2 * h + 1 : 2 * h + 2, :]
        grad_value = dot_nn(probs.astype(BF), grad)
        grad_probs = dot_nt(value, grad_h)
        both = probs * grad_probs
        dots = jnp.sum(both, axis=0, keepdims=True)
        grad_raw = (both - probs * dots).astype(BF)
        grad_key = dot_nn(grad_raw, query) * 0.125
        grad_query_t = dot_nn(key_t, grad_raw) * 0.125
        outs.append((grad_query_t, grad_key, grad_value))
    grad_query = jnp.transpose(jnp.where(iota(outs[0][0].shape, 0) < HDIM, outs[0][0], outs[1][0])).astype(BF)
    grad_key = jnp.where(lane < HDIM, outs[0][1], outs[1][1]).astype(BF)
    grad_value = jnp.where(lane < HDIM, outs[0][2], outs[1][2]).astype(BF)
    gproj_ref[0] = grad_query
    gproj_ref[1] = grad_key
    gproj_ref[2] = grad_value
    more = dot_nt(grad_query, weight_ref[0]) + dot_nt(grad_key, weight_ref[1]) + dot_nt(grad_value, weight_ref[2])

    @pl.when(step == 0)
    def _():
        total_s[...] = sum_ref[...] + more

    @pl.when(step > 0)
    def _():
        total_s[...] += more

    @pl.when(step == pl.num_programs(0) - 1)
    def _():
        half = own_ref.shape[1]
        low = total_s[...].astype(BF)

        @pl.when(place[0] == 0)
        def _():
            own_ref[...] = low[:, :half]
            send_ref[...] = low[:, half:]

        @pl.when(place[0] != 0)
        def _():
            own_ref[...] = low[:, half:]
            send_ref[...] = low[:, :half]


def attend_back(place, proj, grad, stat, weight, grad_sum):
    seq, width = grad.shape
    pairs = width // 128
    shapes = (
        jax.ShapeDtypeStruct((3, seq, width), BF),
        jax.ShapeDtypeStruct((seq, width // 2), BF),
        jax.ShapeDtypeStruct((seq, width // 2), BF),
    )
    return pl.pallas_call(
        attend_back_kernel,
        grid_spec=pltpu.PrefetchScalarGridSpec(
            num_scalar_prefetch=1,
            grid=(pairs,),
            in_specs=[
                pl.BlockSpec((3, seq, 128), lambda i, s: (0, 0, i)),
                pl.BlockSpec((seq, 128), lambda i, s: (0, i)),
                pl.BlockSpec((1, 8, seq), lambda i, s: (i, 0, 0)),
                pl.BlockSpec((3, width, 128), lambda i, s: (0, 0, i)),
                whole((seq, width)),
            ],
            out_specs=[
                pl.BlockSpec((3, seq, 128), lambda i, s: (0, 0, i)),
                whole((seq, width // 2)),
                whole((seq, width // 2)),
            ],
            scratch_shapes=[pltpu.VMEM((seq, width), F32)],
        ),
        out_shape=shapes,
        compiler_params=params(),
        name="attend_back",
    )(place, proj, grad, stat, weight, grad_sum)


def gelu_parts(x):
    size = jnp.abs(x)
    t = 1.0 / (1.0 + (0.3275911 * 0.7071067811865476) * size)
    bell = jnp.exp2(x * x * (-0.5 * LOG2E))
    poly = t * (0.254829592 + t * (-0.284496736 + t * (1.421413741 + t * (-1.453152027 + t * 1.061405429))))
    tail = 0.5 * poly * bell
    phi_sum = jnp.where(x >= 0, 1.0 - tail, tail)
    return x * phi_sum, phi_sum + x * bell * 0.3989422804014327


def norm_parts(v):
    centre = v - jnp.mean(v, axis=-1, keepdims=True)
    spread_of = jnp.mean(centre * centre, axis=-1, keepdims=True)
    scale = lax.rsqrt(spread_of + 1e-12)
    return centre * scale, scale


def norm_back(grad, normal, scale, gain):
    e = grad * gain
    return scale * (e - jnp.mean(e, -1, keepdims=True) - normal * jnp.mean(e * normal, -1, keepdims=True))


def forward_kernel(
    place, att_ref, emb_ref, out_w_ref, vec_ref, cot_ref, in_ref, back_ref,
    low_ref, normal_ref, scale_ref, active_ref, slope_ref, mixed_ref, outer_ref, weights_ref, sums_ref,
):
    step = pl.program_id(0)
    seq = att_ref.shape[0]

    @pl.when(step == 0)
    def _():
        total = emb_ref[...].astype(F32) + dot_nn(att_ref[...], out_w_ref[...])
        normal, scale = norm_parts(total)
        normed = normal * vec_ref[0:1, :] + vec_ref[1:2, :]
        normal_ref[...] = normal
        scale_ref[...] = jnp.broadcast_to(scale, scale_ref.shape)
        low_ref[...] = normed.astype(BF)
        mixed_ref[...] = normed

    inner = dot_nt(low_ref[...], in_ref[...])
    active, slope = gelu_parts(inner)
    active = active.astype(BF)
    active_ref[...] = active
    slope_ref[...] = slope
    mixed_ref[...] += dot_nn(active, back_ref[...])

    @pl.when(step == pl.num_programs(0) - 1)
    def _():
        normal, scale = norm_parts(mixed_ref[...])
        gain, term = vec_ref[2:3, :], vec_ref[3:4, :]
        final = normal * gain
        logit = jnp.sum(final * term, axis=-1, keepdims=True)
        live = (iota((seq, 1), 0) < place[1]).astype(F32)
        rest = jnp.exp(-jnp.abs(logit))
        weights = (jnp.maximum(logit, 0.0) + jnp.log1p(rest)) * live
        weights_ref[...] = jnp.broadcast_to(weights, weights_ref.shape)
        sigmoid = jnp.where(logit >= 0, 1.0, rest) / (1.0 + rest)
        grad_logit = cot_ref[:, 0:1] * live * sigmoid
        grad_final = grad_logit * term
        sums_ref[0:1, :] = jnp.sum(grad_final * normal, axis=0, keepdims=True)
        sums_ref[1:2, :] = jnp.sum(grad_logit * final, axis=0, keepdims=True)
        sums_ref[2:8, :] = jnp.zeros((6, sums_ref.shape[1]), F32)
        grad_mixed = norm_back(grad_final, normal, scale, gain)
        mixed_ref[...] = grad_mixed
        outer_ref[...] = grad_mixed.astype(BF)


def forward(place, att, emb, out_w, vec, cot, in_rows, back_rows):
    seq, width = att.shape
    units = in_rows.shape[0]
    step = 768
    shapes = (
        jax.ShapeDtypeStruct((seq, width), BF),
        jax.ShapeDtypeStruct((seq, width), F32),
        jax.ShapeDtypeStruct((seq, 128), F32),
        jax.ShapeDtypeStruct((seq, units), BF),
        jax.ShapeDtypeStruct((seq, units), F32),
        jax.ShapeDtypeStruct((seq, width), F32),
        jax.ShapeDtypeStruct((seq, width), BF),
        jax.ShapeDtypeStruct((seq, 128), F32),
        jax.ShapeDtypeStruct((8, width), F32),
    )
    return pl.pallas_call(
        forward_kernel,
        grid_spec=pltpu.PrefetchScalarGridSpec(
            num_scalar_prefetch=1,
            grid=(units // step,),
            in_specs=[
                whole((seq, width)),
                whole((seq, width)),
                whole((width, width)),
                whole(vec.shape),
                whole(cot.shape),
                pl.BlockSpec((step, width), lambda i, s: (i, 0)),
                pl.BlockSpec((step, width), lambda i, s: (i, 0)),
            ],
            out_specs=[
                whole((seq, width)),
                whole((seq, width)),
                whole((seq, 128)),
                pl.BlockSpec((seq, step), lambda i, s: (0, i)),
                pl.BlockSpec((seq, step), lambda i, s: (0, i)),
                whole((seq, width)),
                whole((seq, width)),
                whole((seq, 128)),
                whole((8, width)),
            ],
        ),
        out_shape=shapes,
        compiler_params=params(),
        name="forward",
    )(place, att, emb, out_w, vec, cot, in_rows, back_rows)


def backward_kernel(
    outer_ref, mixed_ref, normal_ref, scale_ref, out_w_ref, vec_ref, slope_ref, in_ref, back_ref,
    inner_ref, total_ref, branch_ref, att_ref, sums_ref,
):
    step = pl.program_id(0)
    grad_inner = (dot_nt(outer_ref[...], back_ref[...]) * slope_ref[...]).astype(BF)
    inner_ref[...] = grad_inner
    more = dot_nn(grad_inner, in_ref[...])

    @pl.when(step == 0)
    def _():
        total_ref[...] = mixed_ref[...] + more

    @pl.when(step > 0)
    def _():
        total_ref[...] += more

    @pl.when(step == pl.num_programs(0) - 1)
    def _():
        grad = total_ref[...]
        normal = normal_ref[...]
        sums_ref[0:1, :] = jnp.sum(grad * normal, axis=0, keepdims=True)
        sums_ref[1:2, :] = jnp.sum(grad, axis=0, keepdims=True)
        sums_ref[2:8, :] = jnp.zeros((6, sums_ref.shape[1]), F32)
        grad_sum = norm_back(grad, normal, scale_ref[:, 0:1], vec_ref[0:1, :])
        total_ref[...] = grad_sum
        branch = grad_sum.astype(BF)
        branch_ref[...] = branch
        att_ref[...] = dot_nt(branch, out_w_ref[...]).astype(BF)


def backward(outer, mixed, normal, scale, out_w, vec, slope, in_rows, back_rows):
    seq, width = outer.shape
    units = in_rows.shape[0]
    step = 768
    shapes = (
        jax.ShapeDtypeStruct((seq, units), BF),
        jax.ShapeDtypeStruct((seq, width), F32),
        jax.ShapeDtypeStruct((seq, width), BF),
        jax.ShapeDtypeStruct((seq, width), BF),
        jax.ShapeDtypeStruct((8, width), F32),
    )
    return pl.pallas_call(
        backward_kernel,
        grid=(units // step,),
        in_specs=[
            whole((seq, width)),
            whole((seq, width)),
            whole((seq, width)),
            whole((seq, 128)),
            whole((width, width)),
            whole(vec.shape),
            pl.BlockSpec((seq, step), lambda i: (0, i)),
            pl.BlockSpec((step, width), lambda i: (i, 0)),
            pl.BlockSpec((step, width), lambda i: (i, 0)),
        ],
        out_specs=[
            pl.BlockSpec((seq, step), lambda i: (0, i)),
            whole((seq, width)),
            whole((seq, width)),
            whole((seq, width)),
            whole((8, width)),
        ],
        out_shape=shapes,
        compiler_params=params(),
        name="backward",
    )(outer, mixed, normal, scale, out_w, vec, slope, in_rows, back_rows)


def unit_grad_kernel(keep_in, send_in, other_ref, keep_ref, send_ref):
    for source, out in ((send_in, send_ref), (keep_in, keep_ref)):
        out[...] = dot_tn(source[...], other_ref[...]).astype(BF).reshape(out.shape)


def unit_grad(rows, other, swap):
    seq, units = rows.shape
    width = other.shape[1]
    step = units // 4
    if swap:
        spec = pl.BlockSpec((2, 1, step // 2, width), lambda i: (0, i, 0, 0))
        shape = jax.ShapeDtypeStruct((2, 2, step // 2, width), BF)
    else:
        spec = pl.BlockSpec((1, 2, step // 2, width), lambda i: (i, 0, 0, 0))
        shape = jax.ShapeDtypeStruct((2, 2, step // 2, width), BF)
    keep, send = pl.pallas_call(
        unit_grad_kernel,
        grid=(2,),
        in_specs=[
            pl.BlockSpec((seq, step), lambda i: (0, i)),
            pl.BlockSpec((seq, step), lambda i: (0, 2 + i)),
            whole((seq, width)),
        ],
        out_specs=[spec, spec],
        out_shape=[shape, shape],
        compiler_params=params(),
        name="unit_grad",
    )(rows, rows, other)
    return keep.reshape(units // 2, width), send.reshape(units // 2, width)


def out_grad_kernel(order_ref, branch_ref, att_ref, first_ref, second_ref, keep_ref, send_ref):
    width = att_ref.shape[1]
    half = keep_ref.shape[0]
    hot = (iota((width, width), 0) == order_ref[0:1, :]).astype(F32).astype(BF)
    moved = dot_nn(branch_ref[...], hot).astype(BF)
    grad = dot_tn(moved, att_ref[...]).astype(BF)
    lines = jnp.concatenate([first_ref[...], second_ref[...], jnp.zeros((112, width), F32)], axis=0).astype(BF)
    sums = jnp.transpose(dot_nn(lines, hot)).astype(BF)
    keep_ref[:, :width] = grad[:half]
    send_ref[:, :width] = grad[half:]
    keep_ref[:, width:] = sums[:half]
    send_ref[:, width:] = sums[half:]


def out_grad(order, branch, att, first, second):
    width = att.shape[1]
    shape = jax.ShapeDtypeStruct((width // 2, width + 128), BF)
    args = (order, branch, att, first, second)
    return pl.pallas_call(
        out_grad_kernel,
        grid=(1,),
        in_specs=[whole(a.shape) for a in args],
        out_specs=[whole(shape.shape)] * 2,
        out_shape=[shape] * 2,
        compiler_params=params(),
        name="out_grad",
    )(*args)


def proj_grad_kernel(place, order_ref, emb_ref, keep_in, send_in, keep_ref, send_ref, moved_s):
    width = emb_ref.shape[1]

    @pl.when(pl.program_id(0) == 0)
    def _():
        hot = (iota((width, width), 0) == order_ref[0:1, :]).astype(F32).astype(BF)
        moved_s[...] = dot_nn(emb_ref[...], hot).astype(BF)

    for source, out in ((send_in, send_ref), (keep_in, keep_ref)):
        out[...] = dot_tn(moved_s[...], source[0]).astype(BF)


def proj_grad(place, order, emb, gproj):
    seq, width = emb.shape
    half = width // 2
    shape = jax.ShapeDtypeStruct((width, 3 * half), BF)
    return pl.pallas_call(
        proj_grad_kernel,
        grid_spec=pltpu.PrefetchScalarGridSpec(
            num_scalar_prefetch=1,
            grid=(3,),
            in_specs=[
                whole(order.shape),
                whole(emb.shape),
                pl.BlockSpec((1, seq, half), lambda i, s: (i, 0, s[0])),
                pl.BlockSpec((1, seq, half), lambda i, s: (i, 0, 1 - s[0])),
            ],
            out_specs=[pl.BlockSpec((width, half), lambda i, s: (0, i))] * 2,
            scratch_shapes=[pltpu.VMEM((seq, width), BF)],
        ),
        out_shape=[shape] * 2,
        compiler_params=params(),
        name="proj_grad",
    )(place, order, emb, gproj, gproj)


def swap_head(x):
    return lax.ppermute(x, "head", [(0, 1), (1, 0)])


def swap_dp(x, bit):
    return lax.ppermute(x, "dp", [(i, i ^ bit) for i in range(lax.axis_size("dp"))])


def scatter_sum(keep, recv, bits):
    for bit in bits:
        half = keep.shape[0] // 2
        out = keep[half:] + recv[half:]
        keep = keep[:half] + recv[:half]
        recv = swap_dp(out, bit)
    return keep.astype(F32) + recv.astype(F32)


def reversed_bits(count):
    bits = count.bit_length() - 1
    return [sum(((i >> b) & 1) << (bits - 1 - b) for b in range(bits)) for i in range(count)]


def swap_low(i):
    return (i & ~3) | ((i & 1) << 1) | ((i >> 1) & 1)


def body(
    token_ids,
    lengths,
    embed_table,
    qkv_weight,
    out_weight,
    first_gain,
    first_bias,
    in_weight,
    back_weight,
    second_gain,
    term_vector,
    cotangent,
):
    dp = lax.axis_index("dp")
    head = lax.axis_index("head")
    owners = lax.axis_size("dp")
    bits = [1 << b for b in range(owners.bit_length() - 1)]
    other_bits = [2, 1] + bits[2:]
    device = dp * 2 + head
    seq = token_ids.shape[0]
    table_rows, half = embed_table.shape
    width = 2 * half
    units = back_weight.shape[0]
    cap = 4 * seq // owners
    slots = owners * cap

    ids = token_ids.reshape(1, seq)
    ids = jnp.concatenate([ids, swap_head(ids)], axis=1)
    for bit in bits:
        ids = jnp.concatenate([ids, swap_dp(ids, bit)], axis=0)
    picked, asked, slot_row, slot_col = pick(dp.reshape(1), ids, embed_table, cap)
    got = lax.all_to_all(picked.reshape(owners, cap, half), "dp", split_axis=0, concat_axis=0, tiled=True)

    unit_order = device ^ jnp.array(reversed_bits(2 * owners), jnp.int32)
    back_rows = jnp.take(back_weight.reshape(2 * owners, -1, width), unit_order, axis=0).reshape(units, width)
    in_rows = jnp.take(in_weight.T.reshape(2 * owners, -1, width), unit_order, axis=0).reshape(units, width)
    other_weight = swap_head(qkv_weight)
    weight = jnp.where(
        head == 0,
        jnp.concatenate([qkv_weight, other_weight], axis=2),
        jnp.concatenate([other_weight, qkv_weight], axis=2),
    )
    out_block = width // (2 * owners)
    out_order = (unit_order[:, None] * out_block + jnp.arange(out_block, dtype=jnp.int32)[None, :]).reshape(1, width)
    row_block = width // owners // 2
    rev = reversed_bits(owners)
    first_half = (dp ^ jnp.array(rev, jnp.int32))[:, None] * (2 * row_block) + jnp.arange(row_block, dtype=jnp.int32)
    second_half = (dp ^ jnp.array([swap_low(r) for r in rev], jnp.int32))[:, None] * (2 * row_block) + (
        row_block + jnp.arange(row_block, dtype=jnp.int32)
    )
    proj_order = jnp.concatenate([first_half.reshape(1, half), second_half.reshape(1, half)], axis=1)
    vec = jnp.concatenate(
        [jnp.stack([first_gain, first_bias, second_gain, term_vector]), jnp.zeros((4, width), F32)], axis=0
    )
    cot = jnp.broadcast_to(cotangent.reshape(seq, 1), (seq, 128))
    place = jnp.stack([head, lengths[0]]).astype(jnp.int32)

    own, send = regather(slot_col, got.reshape(slots, half))
    other = swap_head(send)
    emb, proj, att, stat = attend(place, own, other, weight)
    low, normal, scale, active, slope, mixed, outer, weights, sums_two = forward(
        place, att, emb, out_weight, vec, cot, in_rows, back_rows
    )
    back_keep, back_send = unit_grad(active, outer, True)
    back_recv = swap_head(back_send)
    grad_inner, grad_sum, branch, grad_att, sums_one = backward(
        outer, mixed, normal, scale, out_weight, vec, slope, in_rows, back_rows
    )
    in_keep, in_send = unit_grad(grad_inner, low, False)
    in_recv = swap_head(in_send)
    grad_back = scatter_sum(back_keep, back_recv, other_bits)
    grad_in = scatter_sum(in_keep, in_recv, bits)
    gproj, grad_own, grad_send = attend_back(place, proj, grad_att, stat, weight, grad_sum)
    grad_other = swap_head(grad_send)
    sent = spread(slot_row, grad_own, grad_other, slots)
    arrived = lax.all_to_all(sent.reshape(owners, cap, half), "dp", split_axis=0, concat_axis=0, tiled=True)
    out_keep, out_send = out_grad(out_order, branch, att, sums_one, sums_two)
    grad_out = scatter_sum(out_keep, swap_head(out_send), bits)
    proj_keep, proj_send = proj_grad(place, proj_order, emb, gproj)
    proj_recv = swap_head(proj_send)
    grad_first = scatter_sum(proj_keep[:half], proj_recv[:half], bits)
    grad_second = scatter_sum(proj_keep[half:], proj_recv[half:], other_bits)
    grad_table = table_grad(asked.reshape(slots // 512, 512), arrived.reshape(slots, half), table_rows)
    grad_qkv = jnp.concatenate([grad_first, grad_second], axis=0)
    grad_qkv = grad_qkv.reshape(-1, 3, half).transpose(1, 0, 2)
    vectors = grad_out[:, width:]
    return (
        weights[:, 0],
        grad_table,
        grad_qkv,
        grad_out[:, :width].T,
        grad_in.T,
        grad_back,
        vectors[:, 0],
        vectors[:, 1],
        vectors[:, 8],
        vectors[:, 9],
    )


def solution(mesh):
    in_specs = (
        P(("dp", "head")),
        P(("dp", "head")),
        P("dp", "head"),
        P(None, None, "head"),
        P(),
        P(),
        P(),
        P(),
        P(),
        P(),
        P(),
        P(("dp", "head")),
    )
    out_specs = (
        P(("dp", "head")),
        P("dp", "head"),
        P(None, "dp", "head"),
        P(None, ("dp", "head")),
        P(None, ("dp", "head")),
        P(("dp", "head"), None),
        P(("dp", "head")),
        P(("dp", "head")),
        P(("dp", "head")),
        P(("dp", "head")),
    )
    return jax.shard_map(body, mesh=mesh, in_specs=in_specs, out_specs=out_specs, check_vma=False)
```

```python
import functools

import jax
import jax.numpy as jnp
from jax import lax
from jax.experimental import pallas as pl
from jax.experimental.pallas import tpu as pltpu
from jax.sharding import PartitionSpec as P

HDIM = 64
LOG2E = 1.4426950408889634
BF = jnp.bfloat16
F32 = jnp.float32
VMEM_LIMIT = 40 * 1024 * 1024


def dot_nn(a, b):
    return lax.dot_general(a, b, (((1,), (0,)), ((), ())), preferred_element_type=F32)


def dot_nt(a, b):
    return lax.dot_general(a, b, (((1,), (1,)), ((), ())), preferred_element_type=F32)


def dot_tn(a, b):
    return lax.dot_general(a, b, (((0,), (0,)), ((), ())), preferred_element_type=F32)


def iota(shape, dim):
    return lax.broadcasted_iota(jnp.int32, shape, dim)


def params(**more):
    return pltpu.CompilerParams(vmem_limit_bytes=VMEM_LIMIT, **more)


def whole(shape):
    return pl.BlockSpec(shape, lambda *_: (0,) * len(shape))


def cost(micros):
    return pl.CostEstimate(flops=0, bytes_accessed=int(micros * 1e3), transcendentals=0)


ANY = pl.BlockSpec(memory_space=pl.ANY)


def run(kernel, name, micros, scalars, args, grid, in_specs, out_specs, shapes, scratch=(), after=()):
    first, count = len(scalars) + len(args), len(after)

    def inner(*refs):
        kernel(*refs[:first], *refs[first + count :])

    return pl.pallas_call(
        inner,
        grid_spec=pltpu.PrefetchScalarGridSpec(
            num_scalar_prefetch=len(scalars),
            grid=grid,
            in_specs=list(in_specs) + [ANY] * count,
            out_specs=out_specs,
            scratch_shapes=list(scratch),
        ),
        out_shape=shapes,
        compiler_params=params(),
        cost_estimate=cost(micros),
        name=name,
    )(*scalars, *args, *after)


def pick_kernel(place, ids_ref, table_ref, picked_ref, asked_ref, row_ref, col_ref, rank_s, away_s, hot_s):
    owners, block = ids_ref.shape
    rows = table_ref.shape[0]
    cap = picked_ref.shape[0] // owners
    dp = place[0]
    ids = ids_ref[...]
    away = ids - dp * rows
    mine = (away >= 0) & (away < rows)
    floor = iota((owners, block), 0) * rows
    own_ids = ids_ref[0:1, :]
    marks = (own_ids >= floor) & (own_ids < floor + rows)
    both = jnp.concatenate([mine.astype(F32), marks.astype(F32)], axis=0).astype(BF)
    upto = (iota((block, block), 0) <= iota((block, block), 1)).astype(F32).astype(BF)
    counts = dot_nn(both, upto)
    rank_s[...] = (jnp.where(mine, counts[:owners], 0.0) - 1.0).astype(jnp.int32)
    away_s[...] = away
    spot = jnp.where(marks, counts[owners:] - 1.0 + iota((owners, block), 0).astype(F32) * cap, 0.0)
    slot = jnp.sum(spot, axis=0, keepdims=True)
    row_ref[...] = jnp.broadcast_to(slot, row_ref.shape)
    col_ref[...] = jnp.transpose(jnp.broadcast_to(slot, (128, block)))
    group = hot_s.shape[0] // cap
    spots = iota((cap, block), 0)
    lanes = iota((cap, 128), 1)

    def per_group(g, table_of):
        for i in range(group):
            j = g * group + i
            r = j ^ dp
            found = jnp.where(spots == rank_s[pl.ds(r, 1), :], away_s[pl.ds(r, 1), :], 0)
            asked = jnp.sum(found, axis=1, keepdims=True)
            table_of = jnp.where(lanes == j, asked, table_of)
            hot_s[i * cap : (i + 1) * cap, :] = (iota((cap, rows), 1) == asked).astype(F32).astype(BF)
        size = group * cap
        picked_ref[pl.ds(pl.multiple_of(g * size, size), size), :] = dot_nn(hot_s[...], table_ref[...]).astype(BF)
        return table_of

    table_of = lax.fori_loop(0, owners // group, per_group, jnp.zeros((cap, 128), jnp.int32))
    asked_ref[...] = jnp.transpose(table_of.astype(F32))


def pick(dp, ids, table, cap):
    owners, block = ids.shape
    rows, half = table.shape
    group = min(owners, max(1, 512 // cap))
    shapes = (
        jax.ShapeDtypeStruct((owners * cap, half), BF),
        jax.ShapeDtypeStruct((128, cap), F32),
        jax.ShapeDtypeStruct((8, block), F32),
        jax.ShapeDtypeStruct((block, 128), F32),
    )
    return run(
        pick_kernel, "pick", 9, (dp,), (ids, table), (1,),
        [whole(ids.shape), whole(table.shape)],
        [whole(s.shape) for s in shapes],
        shapes,
        [pltpu.VMEM((owners, block), jnp.int32)] * 2 + [pltpu.VMEM((group * cap, rows), BF)],
    )


def regather_kernel(col_ref, got_ref, own_ref, send_ref):
    slots = got_ref.shape[0]
    half = own_ref.shape[0]
    for part, out in ((1, send_ref), (0, own_ref)):
        slot = col_ref[part * half : (part + 1) * half, 0:1].astype(jnp.int32)
        hot = (iota((half, slots), 1) == slot).astype(F32).astype(BF)
        out[...] = dot_nn(hot, got_ref[...]).astype(BF)


def regather(col, got, after):
    block, half = col.shape[0], got.shape[1]
    shapes = [jax.ShapeDtypeStruct((block // 2, half), BF)] * 2
    return run(
        regather_kernel, "regather", 2.5, (), (col, got), (1,),
        [whole(col.shape), whole(got.shape)], [whole(s.shape) for s in shapes], shapes, (), after,
    )


def spread_kernel(row_ref, own_ref, other_ref, out_ref):
    half = own_ref.shape[0]
    step = out_ref.shape[0]
    base = pl.program_id(0) * step
    slot = row_ref[0:1, :].astype(jnp.int32)
    place = iota((step, half), 0) + base
    hot_own = (place == slot[:, :half]).astype(F32).astype(BF)
    hot_other = (place == slot[:, half:]).astype(F32).astype(BF)
    out_ref[...] = (dot_nn(hot_own, own_ref[...]) + dot_nn(hot_other, other_ref[...])).astype(BF)


def spread(row, own, other, slots, after):
    step = 512
    return run(
        spread_kernel, "spread", 3.7, (), (row, own, other), (slots // step,),
        [whole(row.shape), whole(own.shape), whole(other.shape)],
        pl.BlockSpec((step, own.shape[1]), lambda i: (i, 0)),
        jax.ShapeDtypeStruct((slots, own.shape[1]), BF),
        (),
        after,
    )


def table_kernel(asked_ref, got_ref, out_ref):
    step = out_ref.shape[0]
    base = pl.program_id(0) * step
    total = jnp.zeros(out_ref.shape, F32)
    lines, width = asked_ref.shape
    for c in range(lines):
        asked = asked_ref[c : c + 1, :].astype(jnp.int32)
        hot = (iota((step, width), 0) + base == asked).astype(F32).astype(BF)
        total = total + dot_nn(hot, got_ref[c * width : (c + 1) * width, :])
    out_ref[...] = total


def table_grad(asked, got, rows, after):
    step = 640 if rows % 640 == 0 else rows
    return run(
        table_kernel, "table_grad", 5.5, (), (asked, got), (rows // step,),
        [whole(asked.shape), whole(got.shape)],
        pl.BlockSpec((step, got.shape[1]), lambda i: (i, 0)),
        jax.ShapeDtypeStruct((rows, got.shape[1]), F32),
        (),
        after,
    )


def pair_of(i, s, count):
    return jnp.where(i < count, s[0] * count + i, (1 - s[0]) * count + i - count)


def head_views(key, query, length):
    lane = iota(query.shape, 1)
    dead = jnp.where(iota(key.shape, 0) < length, 0.0, -1e30).astype(BF)
    one, zero = jnp.ones_like(query), jnp.zeros_like(query)
    for h in range(2):
        spare = HDIM if h == 0 else 0
        this = (lane < HDIM) if h == 0 else (lane >= HDIM)
        yield this, jnp.where(lane == spare, dead, key), jnp.where(this, query, jnp.where(lane == spare, one, zero))


def attend_kernel(place, own_ref, other_ref, mine_ref, theirs_ref, emb_ref, proj_ref, out_ref, stat_ref):
    half = own_ref.shape[1]
    step = pl.program_id(0)

    @pl.when(step == 0)
    def _():
        @pl.when(place[0] == 0)
        def _():
            emb_ref[:, :half] = own_ref[...]
            emb_ref[:, half:] = other_ref[...]

        @pl.when(place[0] != 0)
        def _():
            emb_ref[:, :half] = other_ref[...]
            emb_ref[:, half:] = own_ref[...]

    weight = jnp.where(step < half // 128, mine_ref[...], theirs_ref[...])
    weight = jnp.concatenate([weight[0], weight[1], weight[2]], axis=1)
    proj = dot_nn(emb_ref[...], weight).astype(BF)
    query, key, value = proj[:, :128], proj[:, 128:256], proj[:, 256:]
    proj_ref[0] = query
    proj_ref[1] = key
    proj_ref[2] = value
    value_t = jnp.transpose(value)
    parts = []
    for h, (_, keys, queries) in enumerate(head_views(key, query, place[1])):
        score = dot_nt(keys, queries)
        top = jnp.max(score, axis=0, keepdims=True) * (0.125 * LOG2E)
        power = jnp.exp2(score * (0.125 * LOG2E) - top)
        total = jnp.sum(power, axis=0, keepdims=True)
        stat_ref[0, h : h + 1, :] = top + jnp.log2(total)
        parts.append(dot_nn(value_t[h * HDIM : (h + 1) * HDIM], power.astype(BF)) * (1.0 / total))
    out_ref[...] = jnp.transpose(jnp.concatenate(parts, axis=0)).astype(BF)


def attend(place, own, other, mine, theirs):
    seq, half = own.shape
    width = 2 * half
    pairs = width // 128
    count = pairs // 2
    shapes = (
        jax.ShapeDtypeStruct((seq, width), BF),
        jax.ShapeDtypeStruct((3, seq, width), BF),
        jax.ShapeDtypeStruct((seq, width), BF),
        jax.ShapeDtypeStruct((pairs, 8, seq), F32),
    )
    return run(
        attend_kernel, "attend", 12, (place,), (own, other, mine, theirs), (pairs,),
        [
            whole(own.shape),
            whole(other.shape),
            pl.BlockSpec((3, width, 128), lambda i, s: (0, 0, jnp.minimum(i, count - 1))),
            pl.BlockSpec((3, width, 128), lambda i, s: (0, 0, jnp.maximum(i - count, 0))),
        ],
        [
            whole((seq, width)),
            pl.BlockSpec((3, seq, 128), lambda i, s: (0, 0, i)),
            pl.BlockSpec((seq, 128), lambda i, s: (0, pair_of(i, s, count))),
            pl.BlockSpec((1, 8, seq), lambda i, s: (i, 0, 0)),
        ],
        shapes,
    )


def attend_back_kernel(last, place, proj_ref, grad_ref, stat_ref, weight_ref, sum_ref, gproj_ref, *outs):
    step = pl.program_id(0)
    query, key, value = proj_ref[0], proj_ref[1], proj_ref[2]
    grad = grad_ref[...]
    lane = iota(query.shape, 1)
    key_t = jnp.transpose(key)
    queries_t, grads_k, grads_v = [], [], []
    for h, (this, keys, queries) in enumerate(head_views(key, query, place[1])):
        score = dot_nt(keys, queries)
        probs = jnp.exp2(score * (0.125 * LOG2E) - stat_ref[0, h : h + 1, :])
        grads_v.append(dot_nn(probs.astype(BF), grad))
        grad_probs = dot_nt(value, jnp.where(this, grad, jnp.zeros_like(grad)))
        dots = jnp.sum(probs * grad_probs, axis=0, keepdims=True)
        grad_raw = (probs * (grad_probs - dots)).astype(BF)
        grads_k.append(dot_nn(grad_raw, query))
        queries_t.append(dot_nn(key_t[h * HDIM : (h + 1) * HDIM], grad_raw))
    grad_query = (jnp.transpose(jnp.concatenate(queries_t, axis=0)) * 0.125).astype(BF)
    grad_key = (jnp.where(lane < HDIM, grads_k[0], grads_k[1]) * 0.125).astype(BF)
    grad_value = jnp.where(lane < HDIM, grads_v[0], grads_v[1]).astype(BF)
    gproj_ref[0] = grad_query
    gproj_ref[1] = grad_key
    gproj_ref[2] = grad_value
    weight = weight_ref[...]
    weight = jnp.concatenate([weight[0], weight[1], weight[2]], axis=1)
    more = dot_nt(jnp.concatenate([grad_query, grad_key, grad_value], axis=1), weight)
    total = outs[-1]

    @pl.when(step == 0)
    def _():
        total[...] = sum_ref[...] + more

    @pl.when(step > 0)
    def _():
        total[...] += more

    if last:
        own_ref, send_ref = outs[:2]
        half = own_ref.shape[1]

        @pl.when(step == pl.num_programs(0) - 1)
        def _():
            low = total[...].astype(BF)

            @pl.when(place[0] == 0)
            def _():
                own_ref[...] = low[:, :half]
                send_ref[...] = low[:, half:]

            @pl.when(place[0] != 0)
            def _():
                own_ref[...] = low[:, half:]
                send_ref[...] = low[:, :half]


def attend_back(place, proj, grad, stat, weight, grad_sum, mine, after):
    seq, width = grad.shape
    half = width // 2
    count = half // 128
    base = 0 if mine else count
    gproj = jax.ShapeDtypeStruct((3, seq, half), BF)
    part = jax.ShapeDtypeStruct((seq, half), BF)
    total = jax.ShapeDtypeStruct((seq, width), F32)
    out_specs = [pl.BlockSpec((3, seq, 128), lambda i, s: (0, 0, i))]
    return run(
        functools.partial(attend_back_kernel, mine), "attend_back", 9, (place,),
        (proj, grad, stat, weight, grad_sum), (count,),
        [
            pl.BlockSpec((3, seq, 128), lambda i, s: (0, 0, i + base)),
            pl.BlockSpec((seq, 128), lambda i, s: (0, pair_of(i + base, s, count))),
            pl.BlockSpec((1, 8, seq), lambda i, s: (i + base, 0, 0)),
            pl.BlockSpec((3, width, 128), lambda i, s: (0, 0, i)),
            whole((seq, width)),
        ],
        out_specs + ([whole(part.shape)] * 2 if mine else [whole(total.shape)]),
        [gproj] + ([part] * 2 if mine else [total]),
        [pltpu.VMEM((seq, width), F32)] if mine else [],
        after,
    )


def gelu_parts(x):
    size = jnp.abs(x)
    t = 1.0 / (1.0 + (0.3275911 * 0.7071067811865476) * size)
    bell = jnp.exp2(x * x * (-0.5 * LOG2E))
    poly = t * (0.254829592 + t * (-0.284496736 + t * (1.421413741 + t * (-1.453152027 + t * 1.061405429))))
    tail = 0.5 * poly * bell
    phi_sum = jnp.where(x >= 0, 1.0 - tail, tail)
    return x * phi_sum, phi_sum + x * bell * 0.3989422804014327


def norm_parts(v):
    centre = v - jnp.mean(v, axis=-1, keepdims=True)
    spread_of = jnp.mean(centre * centre, axis=-1, keepdims=True)
    scale = lax.rsqrt(spread_of + 1e-12)
    return centre * scale, scale


def norm_back(grad, normal, scale, gain):
    e = grad * gain
    return scale * (e - jnp.mean(e, -1, keepdims=True) - normal * jnp.mean(e * normal, -1, keepdims=True))


def forward_kernel(
    place, att_ref, emb_ref, out_w_ref, vec_ref, cot_ref, in_ref, back_ref,
    low_ref, normal_ref, scale_ref, send_ref, keep_ref, slope_ref, mixed_ref, outer_ref, weights_ref, sums_ref,
):
    step = pl.program_id(0)
    half_steps = pl.num_programs(0) // 2
    seq = att_ref.shape[0]

    @pl.when(step == 0)
    def _():
        total = emb_ref[...].astype(F32) + dot_nn(att_ref[...], out_w_ref[...])
        normal, scale = norm_parts(total)
        normed = normal * vec_ref[0:1, :] + vec_ref[1:2, :]
        normal_ref[...] = normal
        scale_ref[...] = jnp.broadcast_to(scale, scale_ref.shape)
        low_ref[...] = normed.astype(BF)
        mixed_ref[...] = normed

    inner = dot_nt(low_ref[...], in_ref[...])
    active, slope = gelu_parts(inner)
    active = active.astype(BF)
    slope_ref[...] = slope

    @pl.when(step < half_steps)
    def _():
        send_ref[...] = active

    @pl.when(step >= half_steps)
    def _():
        keep_ref[...] = active

    mixed_ref[...] += dot_nn(active, back_ref[...])

    @pl.when(step == pl.num_programs(0) - 1)
    def _():
        normal, scale = norm_parts(mixed_ref[...])
        gain, term = vec_ref[2:3, :], vec_ref[3:4, :]
        final = normal * gain
        logit = jnp.sum(final * term, axis=-1, keepdims=True)
        live = (iota((seq, 1), 0) < place[1]).astype(F32)
        rest = jnp.exp(-jnp.abs(logit))
        weights = (jnp.maximum(logit, 0.0) + jnp.log1p(rest)) * live
        weights_ref[...] = jnp.broadcast_to(weights, weights_ref.shape)
        sigmoid = jnp.where(logit >= 0, 1.0, rest) / (1.0 + rest)
        grad_logit = cot_ref[:, 0:1] * live * sigmoid
        grad_final = grad_logit * term
        sums_ref[0:1, :] = jnp.sum(grad_final * normal, axis=0, keepdims=True)
        sums_ref[1:2, :] = jnp.sum(grad_logit * final, axis=0, keepdims=True)
        sums_ref[2:8, :] = jnp.zeros((6, sums_ref.shape[1]), F32)
        grad_mixed = norm_back(grad_final, normal, scale, gain)
        mixed_ref[...] = grad_mixed
        outer_ref[...] = grad_mixed.astype(BF)


def forward(place, att, emb, out_w, vec, cot, in_rows, back_rows):
    seq, width = att.shape
    units = in_rows.shape[0]
    step = 768
    count = units // step
    part = count // 2
    shapes = (
        jax.ShapeDtypeStruct((seq, width), BF),
        jax.ShapeDtypeStruct((seq, width), F32),
        jax.ShapeDtypeStruct((seq, 128), F32),
        jax.ShapeDtypeStruct((seq, units // 2), BF),
        jax.ShapeDtypeStruct((seq, units // 2), BF),
        jax.ShapeDtypeStruct((seq, units), F32),
        jax.ShapeDtypeStruct((seq, width), F32),
        jax.ShapeDtypeStruct((seq, width), BF),
        jax.ShapeDtypeStruct((seq, 128), F32),
        jax.ShapeDtypeStruct((8, width), F32),
    )
    return run(
        forward_kernel, "forward", 17, (place,), (att, emb, out_w, vec, cot, in_rows, back_rows), (count,),
        [
            whole((seq, width)),
            whole((seq, width)),
            whole((width, width)),
            whole(vec.shape),
            whole(cot.shape),
            pl.BlockSpec((step, width), lambda i, s: (lax.rem(i + part, count), 0)),
            pl.BlockSpec((step, width), lambda i, s: (lax.rem(i + part, count), 0)),
        ],
        [
            whole((seq, width)),
            whole((seq, width)),
            whole((seq, 128)),
            pl.BlockSpec((seq, step), lambda i, s: (0, jnp.minimum(i, part - 1))),
            pl.BlockSpec((seq, step), lambda i, s: (0, jnp.maximum(i - part, 0))),
            pl.BlockSpec((seq, step), lambda i, s: (0, lax.rem(i + part, count))),
            whole((seq, width)),
            whole((seq, width)),
            whole((seq, 128)),
            whole((8, width)),
        ],
        shapes,
    )


def backward_kernel(last, outer_ref, start_ref, slope_ref, in_ref, back_ref, *refs):
    step = pl.program_id(0)
    if last:
        normal_ref, scale_ref, out_w_ref, vec_ref, inner_ref, total_ref, branch_ref, att_ref, sums_ref = refs
    else:
        inner_ref, total_ref = refs
    grad_inner = (dot_nt(outer_ref[...], back_ref[...]) * slope_ref[...]).astype(BF)
    inner_ref[...] = grad_inner
    more = dot_nn(grad_inner, in_ref[...])

    @pl.when(step == 0)
    def _():
        total_ref[...] = start_ref[...] + more

    @pl.when(step > 0)
    def _():
        total_ref[...] += more

    if last:

        @pl.when(step == pl.num_programs(0) - 1)
        def _():
            grad = total_ref[...]
            normal = normal_ref[...]
            sums_ref[0:1, :] = jnp.sum(grad * normal, axis=0, keepdims=True)
            sums_ref[1:2, :] = jnp.sum(grad, axis=0, keepdims=True)
            sums_ref[2:8, :] = jnp.zeros((6, sums_ref.shape[1]), F32)
            grad_sum = norm_back(grad, normal, scale_ref[:, 0:1], vec_ref[0:1, :])
            total_ref[...] = grad_sum
            branch = grad_sum.astype(BF)
            branch_ref[...] = branch
            att_ref[...] = dot_nt(branch, out_w_ref[...]).astype(BF)


def backward(outer, start, slope, in_rows, back_rows, rest, after):
    seq, width = outer.shape
    units = in_rows.shape[0]
    step = 768
    count = units // step // 2
    base = 0 if rest else count
    shapes = [jax.ShapeDtypeStruct((seq, units // 2), BF), jax.ShapeDtypeStruct((seq, width), F32)]
    if rest:
        shapes += [jax.ShapeDtypeStruct((seq, width), BF)] * 2 + [jax.ShapeDtypeStruct((8, width), F32)]
    return run(
        functools.partial(backward_kernel, bool(rest)), "backward", 7, (),
        (outer, start, slope, in_rows, back_rows) + tuple(rest), (count,),
        [
            whole((seq, width)),
            whole((seq, width)),
            pl.BlockSpec((seq, step), lambda i: (0, i + base)),
            pl.BlockSpec((step, width), lambda i: (i + base, 0)),
            pl.BlockSpec((step, width), lambda i: (i + base, 0)),
        ]
        + [whole(r.shape) for r in rest],
        [pl.BlockSpec((seq, step), lambda i: (0, i))] + [whole(x.shape) for x in shapes[1:]],
        shapes,
        (),
        after,
    )


def unit_grad_kernel(own_ref, recv_ref, own_other, recv_other, low_ref, high_ref):
    rows = low_ref.shape[0]
    for i, out in enumerate((high_ref, low_ref)):
        cols = slice((1 - i) * rows, (2 - i) * rows)
        out[...] = (dot_tn(own_ref[:, cols], own_other[...]) + dot_tn(recv_ref[:, cols], recv_other[...])).astype(BF)


def unit_grad(own, recv, own_other, recv_other, after):
    width = own_other.shape[1]
    shape = jax.ShapeDtypeStruct((own.shape[1] // 2, width), BF)
    args = (own, recv, own_other, recv_other)
    return run(
        unit_grad_kernel, "unit_grad", 3, (), args, (1,),
        [whole(a.shape) for a in args], [whole(shape.shape)] * 2, [shape] * 2, (), after,
    )


def side_grad_kernel(
    order_ref, spots_ref, emb_ref, emb_recv, gproj_ref, gproj_recv, branch_ref, branch_recv, att_ref, att_recv,
    sums_ref, sums_recv, low_ref, high_ref,
):
    seq, width = att_ref.shape
    half = width // 2
    rows = half // 2
    outs = (low_ref, high_ref)
    for k in range(2):
        place = order_ref[0:1, k * half : (k + 1) * half]
        hot = (iota((width, half), 0) == place).astype(F32).astype(BF)
        moved = dot_nn(emb_ref[...], hot).astype(BF)
        moved_recv = dot_nn(emb_recv[...], hot).astype(BF)
        for c in range(3):
            grad = (dot_tn(moved, gproj_ref[c]) + dot_tn(moved_recv, gproj_recv[c])).astype(BF)
            at = (3 * k + c) * half
            low_ref[:, at : at + half] = grad[:rows]
            high_ref[:, at : at + half] = grad[rows:]
    hot = (iota((width, half), 0) == spots_ref[0:1, :]).astype(F32).astype(BF)
    moved = dot_nn(branch_ref[...], hot).astype(BF)
    moved_recv = dot_nn(branch_recv[...], hot).astype(BF)
    grad = (dot_tn(moved, att_ref[...]) + dot_tn(moved_recv, att_recv[...])).astype(BF)
    lines = jnp.concatenate([sums_ref[...] + sums_recv[...], jnp.zeros((112, width), F32)], axis=0).astype(BF)
    sums = jnp.transpose(dot_nn(lines, hot)).astype(BF)
    for i, out in enumerate(outs):
        out[:, 6 * half : 8 * half] = grad[i * rows : (i + 1) * rows]
        out[:, 8 * half :] = sums[i * rows : (i + 1) * rows]


def side_grad(*args, after):
    width = args[2].shape[1]
    half = width // 2
    shapes = [jax.ShapeDtypeStruct((half // 2, 8 * half + 128), BF)] * 2
    return run(
        side_grad_kernel, "side_grad", 6, (), args, (1,),
        [whole(a.shape) for a in args], [whole(x.shape) for x in shapes], shapes, (), after,
    )


def swap_head(x):
    return lax.ppermute(x, "head", [(0, 1), (1, 0)])


def swap_dp(x, bit):
    return lax.ppermute(x, "dp", [(i, i ^ bit) for i in range(lax.axis_size("dp"))])


def swap_both(x, bits):
    count = lax.axis_size("dp")
    pairs = [(2 * i + h, 2 * (i ^ bits[h]) + h) for i in range(count) for h in range(2)]
    return lax.ppermute(x, ("dp", "head"), pairs)


def add_kernel(keep_low, keep_high, recv_low, recv_high, send, keep):
    send[...] = keep_high[...] + recv_high[...]
    keep[...] = keep_low[...] + recv_low[...]


def add_halves(keep, recv, after=()):
    if isinstance(keep, tuple):
        half, width = keep[0].shape
    else:
        half, width = keep.shape[0] // 2, keep.shape[1]
        if half % 16:
            total = keep + recv
            return total[half:], total[:half]
    steps = 2 if half % 32 == 0 and half >= 384 else 1
    block = half // steps
    low = pl.BlockSpec((block, width), lambda i: (i, 0))
    high = pl.BlockSpec((block, width), lambda i: (i + steps, 0))
    args, specs = [], []
    for x in (keep, recv):
        args += list(x) if isinstance(x, tuple) else [x, x]
        specs += [low, low] if isinstance(x, tuple) else [low, high]
    shape = jax.ShapeDtypeStruct((half, width), BF)
    return run(add_kernel, "add_halves", 1, (), args, (steps,), specs, [low, low], [shape, shape], (), after)


class Sum:
    def __init__(self, bits, low, high):
        self.bits, self.keep, self.done = bits, low, 0
        self.swap(high)

    def swap(self, send):
        k = self.done
        if k < 2:
            self.recv = swap_both(send, (self.bits[0], self.bits[1]) if k == 0 else (self.bits[1], self.bits[0]))
        else:
            self.recv = swap_dp(send, self.bits[k])
        self.done += 1

    def step(self, after=()):
        send, self.keep = add_halves(self.keep, self.recv, after)
        self.swap(send)
        return self.keep

    def result(self):
        return self.keep.astype(F32) + self.recv.astype(F32)


def reversed_bits(count):
    bits = count.bit_length() - 1
    return [sum(((i >> b) & 1) << (bits - 1 - b) for b in range(bits)) for i in range(count)]


def swap_low(i):
    return (i & ~3) | ((i & 1) << 1) | ((i >> 1) & 1)


def body(
    token_ids,
    lengths,
    embed_table,
    qkv_weight,
    out_weight,
    first_gain,
    first_bias,
    in_weight,
    back_weight,
    second_gain,
    term_vector,
    cotangent,
):
    dp = lax.axis_index("dp")
    head = lax.axis_index("head")
    owners = lax.axis_size("dp")
    bits = [1 << b for b in range(owners.bit_length() - 1)]
    device = dp * 2 + head
    seq = token_ids.shape[0]
    table_rows, half = embed_table.shape
    width = 2 * half
    units = back_weight.shape[0]
    cap = 4 * seq // owners
    slots = owners * cap

    ids = token_ids.reshape(1, seq)
    ids = jnp.concatenate([ids, swap_head(ids)], axis=1)
    for low, high in zip(bits[::2], bits[1::2] + [0]):
        parts = [swap_dp(ids, b) for b in ((low, high, low + high) if high else (low,))]
        ids = jnp.concatenate([ids] + parts, axis=0)
    picked, asked, slot_row, slot_col = pick(dp.reshape(1), ids, embed_table, cap)
    got = lax.all_to_all(picked.reshape(owners, cap, half), "dp", split_axis=0, concat_axis=0, tiled=True)

    rev = reversed_bits(owners)
    ways = jnp.array([rev, [swap_low(r) for r in rev]], jnp.int32)
    keep_blocks, send_blocks = (ways[head] ^ dp) * 2 + head, (ways[1 - head] ^ dp) * 2 + 1 - head
    unit_order = jnp.concatenate([keep_blocks, send_blocks])
    back_rows = jnp.take(back_weight.reshape(2 * owners, -1, width), unit_order, axis=0, mode="clip").reshape(units, width)
    in_rows = jnp.take(in_weight.T.reshape(2 * owners, -1, width), unit_order, axis=0, mode="clip").reshape(units, width)
    other_weight = swap_head(qkv_weight)
    out_block = width // (2 * owners)
    inside = jnp.arange(out_block, dtype=jnp.int32)[None, :]
    lines = lambda start: (start[:, None] * out_block + inside).reshape(1, half)
    spots = lines(keep_blocks)
    order = jnp.concatenate([lines(keep_blocks - head), lines(keep_blocks - head + 1)], axis=1)
    vec = jnp.concatenate(
        [jnp.stack([first_gain, first_bias, second_gain, term_vector]), jnp.zeros((4, width), F32)], axis=0
    )
    asked_rows = asked[:owners].reshape(slots // 512, 512)
    cot = jnp.broadcast_to(cotangent.reshape(seq, 1), (seq, 128))
    place = jnp.stack([head, lengths[0]]).astype(jnp.int32)

    own, send = regather(
        slot_col, got.reshape(slots, half),
        (in_rows, back_rows, other_weight, vec, cot, spots, order, asked_rows),
    )
    other = swap_head(send)
    emb, proj, att, stat = attend(place, own, other, qkv_weight, other_weight)
    emb_recv, att_recv = swap_head(emb), swap_head(att)
    low, normal, scale, active_send, active, slope, mixed, outer, weights, sums_two = forward(
        place, att, emb, out_weight, vec, cot, in_rows, back_rows
    )
    low_recv, outer_recv, active_recv = swap_head(low), swap_head(outer), swap_head(active_send)
    inner_send, total = backward(outer, mixed, slope, in_rows, back_rows, (), ())
    inner_recv = swap_head(inner_send)
    back = Sum(bits, *unit_grad(active, active_recv, outer, outer_recv, (total,)))
    inner, grad_sum, branch, grad_att, sums_one = backward(
        outer, total, slope, in_rows, back_rows, (normal, scale, out_weight, vec), (back.keep,)
    )
    sums = jnp.concatenate([sums_one, sums_two], axis=0)
    branch_recv, sums_recv = swap_head(branch), swap_head(sums)
    ins = Sum(bits, *unit_grad(inner, inner_recv, low, low_recv, (grad_sum,)))
    gproj_send, total = attend_back(place, proj, grad_att, stat, other_weight, grad_sum, False, (ins.keep,))
    gproj_recv = swap_head(gproj_send)
    t = back.step((total,))
    gproj, grad_own, grad_send = attend_back(place, proj, grad_att, stat, qkv_weight, total, True, (t,))
    grad_other = swap_head(grad_send)
    t = back.step((grad_own,))
    t = ins.step((t,))
    sent = spread(slot_row, grad_own, grad_other, slots, (t,))
    arrived = lax.all_to_all(sent.reshape(owners, cap, half), "dp", split_axis=0, concat_axis=0, tiled=True)
    side = Sum(
        bits,
        *side_grad(
            order, spots, emb, emb_recv, gproj, gproj_recv, branch, branch_recv, att, att_recv, sums, sums_recv,
            after=(sent,),
        ),
    )
    t = back.step((side.keep,))
    t = ins.step((t,))
    t = side.step((t,))
    t = ins.step((t,))
    while ins.done < len(bits):
        t = ins.step((t,))
    while back.done < len(bits):
        t = back.step((t,))
    grad_table = table_grad(asked_rows, arrived.reshape(slots, half), table_rows, (t,))
    t = grad_table
    while side.done < len(bits):
        t = side.step((t,))
    grad_back, grad_in, side = back.result(), ins.result(), side.result()
    grad_out = side[:, 6 * half : 8 * half]
    grad_qkv = jnp.concatenate([side[:, : 3 * half], side[:, 3 * half : 6 * half]], axis=0)
    grad_qkv = grad_qkv.reshape(-1, 3, half).transpose(1, 0, 2)
    vectors = side[:, 8 * half :]
    return (
        weights[:, 0],
        grad_table,
        grad_qkv,
        grad_out.T,
        grad_in.T,
        grad_back,
        vectors[:, 0],
        vectors[:, 1],
        vectors[:, 8],
        vectors[:, 9],
    )


def solution(mesh):
    in_specs = (
        P(("dp", "head")),
        P(("dp", "head")),
        P("dp", "head"),
        P(None, None, "head"),
        P(),
        P(),
        P(),
        P(),
        P(),
        P(),
        P(),
        P(("dp", "head")),
    )
    out_specs = (
        P(("dp", "head")),
        P("dp", "head"),
        P(None, "dp", "head"),
        P(None, ("dp", "head")),
        P(None, ("dp", "head")),
        P(("dp", "head"), None),
        P(("dp", "head")),
        P(("dp", "head")),
        P(("dp", "head")),
        P(("dp", "head")),
    )
    return jax.shard_map(body, mesh=mesh, in_specs=in_specs, out_specs=out_specs, check_vma=False)
```

```python
import functools

import jax
import jax.numpy as jnp
from jax import lax
from jax.experimental import pallas as pl
from jax.experimental.pallas import tpu as pltpu
from jax.sharding import PartitionSpec as P

HDIM = 64
LOG2E = 1.4426950408889634
BF = jnp.bfloat16
F32 = jnp.float32


def dot_nn(a, b):
    return lax.dot_general(a, b, (((1,), (0,)), ((), ())), preferred_element_type=F32)


def dot_nt(a, b):
    return lax.dot_general(a, b, (((1,), (1,)), ((), ())), preferred_element_type=F32)


def dot_tn(a, b):
    return lax.dot_general(a, b, (((0,), (0,)), ((), ())), preferred_element_type=F32)


def iota(shape, dim):
    return lax.broadcasted_iota(jnp.int32, shape, dim)


def params(mib):
    return pltpu.CompilerParams(vmem_limit_bytes=mib * 1024 * 1024)


def whole(shape):
    return pl.BlockSpec(shape, lambda *_: (0,) * len(shape))


def cost(micros):
    return pl.CostEstimate(flops=0, bytes_accessed=int(micros * 1e3), transcendentals=0)


ANY = pl.BlockSpec(memory_space=pl.ANY)


def run(kernel, name, micros, scalars, args, grid, in_specs, out_specs, shapes, scratch=(), after=(), mib=16):
    first, count = len(scalars) + len(args), len(after)

    def inner(*refs):
        refs = refs[:first] + refs[first + count :]
        spot = first + len(shapes)
        kernel(*refs[:spot], *refs[spot + 1 :])

    *outs, token = pl.pallas_call(
        inner,
        grid_spec=pltpu.PrefetchScalarGridSpec(
            num_scalar_prefetch=len(scalars),
            grid=grid,
            in_specs=list(in_specs) + [ANY] * count,
            out_specs=list(out_specs) + [ANY],
            scratch_shapes=list(scratch),
        ),
        out_shape=list(shapes) + [jax.ShapeDtypeStruct((8, 128), F32)],
        compiler_params=params(mib),
        cost_estimate=cost(micros),
        name=name,
    )(*scalars, *args, *after)
    return outs, token


def pick_kernel(place, ids_ref, table_ref, picked_ref, asked_ref, row_ref, col_ref, rank_s, away_s, hot_s):
    lines, seq = ids_ref.shape
    owners = lines // 2
    rows = table_ref.shape[0]
    cap = picked_ref.shape[0] // owners
    dp, head = place[0], place[1]
    away = ids_ref[...] - dp * rows
    mine = (away >= 0) & (away < rows)
    floor = iota((owners, seq), 0) * rows
    marks = []
    for core in range(2):
        own_ids = ids_ref[pl.ds(2 * dp + core, 1), :]
        marks.append((own_ids >= floor) & (own_ids < floor + rows))
    every = jnp.concatenate([m.astype(F32) for m in [mine] + marks], axis=0).astype(BF)
    upto = (iota((seq, seq), 0) <= iota((seq, seq), 1)).astype(F32).astype(BF)
    counts = dot_nn(every, upto)
    line, other = iota((lines, lines), 0), iota((lines, lines), 1)
    before = ((other == line - 1) & (line % 2 == 1)).astype(F32).astype(BF)
    ends = jnp.broadcast_to(counts[:lines, seq - 1 :], (lines, 128)).astype(BF)
    start = dot_nn(before, ends)[:, 0:1]
    rank_s[...] = (jnp.where(mine, counts[:lines] + start, 0.0) - 1.0).astype(jnp.int32)
    away_s[...] = away
    first, second = counts[lines : lines + owners], counts[lines + owners :]
    base = iota((owners, seq), 0).astype(F32) * cap - 1.0
    slots = [
        jnp.sum(jnp.where(marks[0], first + base, 0.0), axis=0, keepdims=True),
        jnp.sum(jnp.where(marks[1], second + first[:, seq - 1 :] + base, 0.0), axis=0, keepdims=True),
    ]
    own = jnp.where(head == 0, slots[0], slots[1])
    partner = jnp.where(head == 0, slots[1], slots[0])
    slot = jnp.concatenate([own, partner], axis=1)
    row_ref[...] = jnp.broadcast_to(slot, row_ref.shape)
    col_ref[...] = jnp.transpose(jnp.broadcast_to(slot, (128, 2 * seq)))
    group = hot_s.shape[0] // cap
    spots = iota((cap, seq), 0)
    lanes = iota((cap, 128), 1)

    def per_group(g, table_of):
        for i in range(group):
            j = g * group + i
            asked = 0
            for core in range(2):
                here = pl.ds(2 * j + core, 1)
                found = jnp.where(spots == rank_s[here, :], away_s[here, :], 0)
                asked = asked + jnp.sum(found, axis=1, keepdims=True)
            table_of = jnp.where(lanes == j, asked, table_of)
            hot_s[i * cap : (i + 1) * cap, :] = (iota((cap, rows), 1) == asked).astype(F32).astype(BF)
        size = group * cap
        picked_ref[pl.ds(pl.multiple_of(g * size, size), size), :] = dot_nn(hot_s[...], table_ref[...]).astype(BF)
        return table_of

    table_of = lax.fori_loop(0, owners // group, per_group, jnp.zeros((cap, 128), jnp.int32))
    asked_ref[...] = jnp.transpose(table_of.astype(F32))


def pick(place, ids, table, cap):
    lines, seq = ids.shape
    owners = lines // 2
    rows, half = table.shape
    group = min(owners, max(1, 512 // cap))
    shapes = (
        jax.ShapeDtypeStruct((owners * cap, half), BF),
        jax.ShapeDtypeStruct((128, cap), F32),
        jax.ShapeDtypeStruct((8, 2 * seq), F32),
        jax.ShapeDtypeStruct((2 * seq, 128), F32),
    )
    return run(
        pick_kernel, "pick", 9, (place,), (ids, table), (1,),
        [whole(ids.shape), whole(table.shape)],
        [whole(s.shape) for s in shapes],
        shapes,
        [pltpu.VMEM((lines, seq), jnp.int32)] * 2 + [pltpu.VMEM((group * cap, rows), BF)],
    )[0]


def regather_kernel(col_ref, got_ref, out_ref):
    slot = col_ref[:, 0:1].astype(jnp.int32)
    hot = (iota((out_ref.shape[0], got_ref.shape[0]), 1) == slot).astype(F32).astype(BF)
    out_ref[...] = dot_nn(hot, got_ref[...]).astype(BF)


def regather(col, got, part, after):
    half, width = col.shape[0] // 2, got.shape[1]
    shape = jax.ShapeDtypeStruct((half, width), BF)
    (out,), token = run(
        regather_kernel, "regather", 2, (), (col, got), (1,),
        [pl.BlockSpec((half, 128), lambda i: (part, 0)), whole(got.shape)], [whole(shape.shape)], [shape], (), after,
    )
    return out, token


def spread_kernel(row_ref, own_ref, other_ref, out_ref):
    half = own_ref.shape[0]
    step = out_ref.shape[0]
    base = pl.program_id(0) * step
    slot = row_ref[0:1, :].astype(jnp.int32)
    place = iota((step, half), 0) + base
    hot_own = (place == slot[:, :half]).astype(F32).astype(BF)
    hot_other = (place == slot[:, half:]).astype(F32).astype(BF)
    out_ref[...] = (dot_nn(hot_own, own_ref[...]) + dot_nn(hot_other, other_ref[...])).astype(BF)


def spread(row, own, other, slots, after):
    step = 512
    return run(
        spread_kernel, "spread", 3.7, (), (row, own, other), (slots // step,),
        [whole(row.shape), whole(own.shape), whole(other.shape)],
        [pl.BlockSpec((step, own.shape[1]), lambda i: (i, 0))],
        [jax.ShapeDtypeStruct((slots, own.shape[1]), BF)],
        (),
        after,
    )


def table_kernel(asked_ref, got_ref, out_ref):
    step = out_ref.shape[0]
    base = pl.program_id(0) * step
    total = jnp.zeros(out_ref.shape, F32)
    lines, width = asked_ref.shape
    for c in range(lines):
        asked = asked_ref[c : c + 1, :].astype(jnp.int32)
        hot = (iota((step, width), 0) + base == asked).astype(F32).astype(BF)
        total = total + dot_nn(hot, got_ref[c * width : (c + 1) * width, :])
    out_ref[...] = total


def table_grad(asked, got, rows, after):
    step = 640 if rows % 640 == 0 else rows
    return run(
        table_kernel, "table_grad", 5.5, (), (asked, got), (rows // step,),
        [whole(asked.shape), whole(got.shape)],
        [pl.BlockSpec((step, got.shape[1]), lambda i: (i, 0))],
        [jax.ShapeDtypeStruct((rows, got.shape[1]), F32)],
        (),
        after,
    )


SCALE = 0.125 * LOG2E


def head_views(key, query, length):
    lane = iota(query.shape, 1)
    dead = jnp.where(iota(key.shape, 0) < length, 0.0, -1e30).astype(BF)
    one, zero = jnp.ones_like(query), jnp.zeros_like(query)
    views = []
    for h in range(2):
        spare = HDIM if h == 0 else 0
        this = (lane < HDIM) if h == 0 else (lane >= HDIM)
        keys = jnp.where(lane == spare, dead, key)
        queries = jnp.where(this, query, jnp.where(lane == spare, one, zero))
        views.append((this, keys, queries))
    return views


def half_column(place, mine, half):
    return place[0] * half if mine else (1 - place[0]) * half


def attend_kernel(place, own_ref, other_ref, weight_ref, pair_ref, proj_ref, stat_ref):
    half = own_ref.shape[1]
    seq = own_ref.shape[0]

    @pl.when(place[0] == 0)
    def _():
        pair_ref[0, :, :half] = own_ref[...]
        pair_ref[0, :, half:] = other_ref[...]

    @pl.when(place[0] != 0)
    def _():
        pair_ref[0, :, :half] = other_ref[...]
        pair_ref[0, :, half:] = own_ref[...]

    for c in range(3):
        proj_ref[c] = dot_nn(pair_ref[0], weight_ref[c]).astype(BF)
    lane = iota((seq, 128), 1)
    pairs = 2 * half // 128

    def scores_of(p):
        here = slice(p * 128, (p + 1) * 128)
        views = head_views(proj_ref[1, :, here], proj_ref[0, :, here], place[1])
        return [dot_nt(queries, keys) for _, keys, queries in views]

    stat = jnp.zeros((seq, 128), F32)
    scores = scores_of(0)
    for p in range(pairs):
        later = scores_of(p + 1) if p + 1 < pairs else None
        value = proj_ref[2, :, p * 128 : (p + 1) * 128]
        parts = []
        for h in range(2):
            top = jnp.max(scores[h], axis=1, keepdims=True) * SCALE
            power = jnp.exp2(scores[h] * SCALE - top)
            total = jnp.sum(power, axis=1, keepdims=True)
            stat = jnp.where(lane == 2 * p + h, top + jnp.log2(total), stat)
            parts.append(dot_nn(power.astype(BF), value) * (1.0 / total))
        mine = p < pairs // 2
        column = half_column(place, mine, half) + (p if mine else p - pairs // 2) * 128
        spot = pl.ds(pl.multiple_of(column, 128), 128)
        pair_ref[1, :, spot] = jnp.where(lane < HDIM, parts[0], parts[1]).astype(BF)
        scores = later
    stat_ref[...] = stat


def attend(place, own, other, weight):
    seq, half = own.shape
    width = 2 * half
    shapes = (
        jax.ShapeDtypeStruct((2, seq, width), BF),
        jax.ShapeDtypeStruct((3, seq, width), BF),
        jax.ShapeDtypeStruct((seq, 128), F32),
    )
    args = (own, other, weight)
    return run(
        attend_kernel, "attend", 9, (place,), args, (1,),
        [whole(a.shape) for a in args], [whole(x.shape) for x in shapes], shapes, mib=32,
    )


def attend_back_kernel(mine, place, proj_ref, grad_ref, stat_ref, weight_ref, sum_ref, gproj_ref, *outs):
    seq, width = grad_ref.shape
    half = width // 2
    base = 0 if mine else half
    column = half_column(place, mine, half)
    lane = iota((seq, 128), 1)
    stat = stat_ref[...]
    for p in range(half // 128):
        here = slice(base + p * 128, base + (p + 1) * 128)
        query, key, value = proj_ref[0, :, here], proj_ref[1, :, here], proj_ref[2, :, here]
        grad = grad_ref[:, pl.ds(pl.multiple_of(column + p * 128, 128), 128)]
        query_t, grad_t = jnp.transpose(query), jnp.transpose(grad)
        grads_q, keys_t, values_t = [], [], []
        for h, (this, keys, queries) in enumerate(head_views(key, query, place[1])):
            rows = slice(h * HDIM, (h + 1) * HDIM)
            at = base // HDIM + 2 * p + h
            probs = jnp.exp2(dot_nt(queries, keys) * SCALE - stat[:, at : at + 1])
            grad_probs = dot_nt(jnp.where(this, grad, jnp.zeros_like(grad)), value)
            values_t.append(dot_nn(grad_t[rows], probs.astype(BF)))
            dots = jnp.sum(probs * grad_probs, axis=1, keepdims=True)
            grad_raw = (probs * (grad_probs - dots)).astype(BF)
            grads_q.append(dot_nn(grad_raw, key))
            keys_t.append(dot_nn(query_t[rows], grad_raw))
        here = slice(p * 128, (p + 1) * 128)
        gproj_ref[0, :, here] = (jnp.where(lane < HDIM, grads_q[0], grads_q[1]) * 0.125).astype(BF)
        gproj_ref[1, :, here] = jnp.transpose((jnp.concatenate(keys_t, axis=0) * 0.125).astype(BF))
        gproj_ref[2, :, here] = jnp.transpose(jnp.concatenate(values_t, axis=0).astype(BF))
    total = sum_ref[...]
    for c in range(3):
        total = total + dot_nt(gproj_ref[c], weight_ref[c, :, base : base + half])
    if not mine:
        outs[0][...] = total
        return
    own_ref, send_ref = outs
    low = total.astype(BF)

    @pl.when(place[0] == 0)
    def _():
        own_ref[...] = low[:, :half]
        send_ref[...] = low[:, half:]

    @pl.when(place[0] != 0)
    def _():
        own_ref[...] = low[:, half:]
        send_ref[...] = low[:, :half]


def attend_back(place, proj, grad, stat, weight, grad_sum, mine, after):
    seq, width = grad.shape
    half = width // 2
    shapes = [jax.ShapeDtypeStruct((3, seq, half), BF)]
    if mine:
        shapes += [jax.ShapeDtypeStruct((seq, half), BF)] * 2
    else:
        shapes += [jax.ShapeDtypeStruct((seq, width), F32)]
    args = (proj, grad, stat, weight, grad_sum)
    return run(
        functools.partial(attend_back_kernel, mine), "attend_back", 9, (place,), args, (1,),
        [whole(a.shape) for a in args], [whole(x.shape) for x in shapes], shapes, (), after, 32,
    )


def gelu_parts(x):
    t = 1.0 / (1.0 + (0.3275911 * 0.7071067811865476) * jnp.abs(x))
    bell = jnp.exp2(x * x * (-0.5 * LOG2E))
    poly = 0.127414796 + t * (-0.142248368 + t * (0.7107068705 + t * (-0.7265760135 + t * 0.5307027145)))
    tail = bell * (t * poly)
    below = jnp.where(x >= 0, 1.0 - tail, tail)
    return x * below, below + x * (bell * 0.3989422804014327)


def norm_parts(v):
    centre = v - jnp.mean(v, axis=-1, keepdims=True)
    spread_of = jnp.mean(centre * centre, axis=-1, keepdims=True)
    scale = lax.rsqrt(spread_of + 1e-12)
    return centre * scale, scale


def norm_back(grad, normal, scale, gain):
    e = grad * gain
    return scale * (e - jnp.mean(e, -1, keepdims=True) - normal * jnp.mean(e * normal, -1, keepdims=True))


def forward_kernel(
    place, pair_ref, out_w_ref, vec_ref, cot_ref, in_ref, back_ref,
    low_ref, normal_ref, scale_ref, send_ref, keep_ref, slope_ref, mixed_ref, outer_ref, weights_ref, sums_ref,
):
    step = pl.program_id(0)
    half_steps = pl.num_programs(0) // 2
    seq = low_ref.shape[0]

    @pl.when(step == 0)
    def _():
        total = pair_ref[0].astype(F32) + dot_nn(pair_ref[1], out_w_ref[...])
        normal, scale = norm_parts(total)
        normed = normal * vec_ref[0:1, :] + vec_ref[1:2, :]
        normal_ref[...] = normal
        scale_ref[...] = jnp.broadcast_to(scale, scale_ref.shape)
        low_ref[...] = normed.astype(BF)
        mixed_ref[...] = normed

    inner = dot_nt(low_ref[...], in_ref[...])
    active, slope = gelu_parts(inner)
    active = active.astype(BF)
    slope_ref[...] = slope

    @pl.when(step < half_steps)
    def _():
        send_ref[...] = active

    @pl.when(step >= half_steps)
    def _():
        keep_ref[...] = active

    mixed_ref[...] += dot_nn(active, back_ref[...])

    @pl.when(step == pl.num_programs(0) - 1)
    def _():
        normal, scale = norm_parts(mixed_ref[...])
        gain, term = vec_ref[2:3, :], vec_ref[3:4, :]
        final = normal * gain
        logit = jnp.sum(final * term, axis=-1, keepdims=True)
        live = (iota((seq, 1), 0) < place[1]).astype(F32)
        rest = jnp.exp(-jnp.abs(logit))
        weights = (jnp.maximum(logit, 0.0) + jnp.log1p(rest)) * live
        weights_ref[...] = jnp.broadcast_to(weights, weights_ref.shape)
        sigmoid = jnp.where(logit >= 0, 1.0, rest) / (1.0 + rest)
        grad_logit = cot_ref[:, 0:1] * live * sigmoid
        grad_final = grad_logit * term
        sums_ref[0:1, :] = jnp.sum(grad_final * normal, axis=0, keepdims=True)
        sums_ref[1:2, :] = jnp.sum(grad_logit * final, axis=0, keepdims=True)
        sums_ref[2:8, :] = jnp.zeros((6, sums_ref.shape[1]), F32)
        grad_mixed = norm_back(grad_final, normal, scale, gain)
        mixed_ref[...] = grad_mixed
        outer_ref[...] = grad_mixed.astype(BF)


def forward(place, pair, out_w, vec, cot, in_rows, back_rows):
    _, seq, width = pair.shape
    units = in_rows.shape[0]
    step = 768
    count = units // step
    part = count // 2
    shapes = (
        jax.ShapeDtypeStruct((seq, width), BF),
        jax.ShapeDtypeStruct((seq, width), F32),
        jax.ShapeDtypeStruct((seq, 128), F32),
        jax.ShapeDtypeStruct((seq, units // 2), BF),
        jax.ShapeDtypeStruct((seq, units // 2), BF),
        jax.ShapeDtypeStruct((seq, units), F32),
        jax.ShapeDtypeStruct((seq, width), F32),
        jax.ShapeDtypeStruct((seq, width), BF),
        jax.ShapeDtypeStruct((seq, 128), F32),
        jax.ShapeDtypeStruct((8, width), F32),
    )
    return run(
        forward_kernel, "forward", 17, (place,), (pair, out_w, vec, cot, in_rows, back_rows), (count,),
        [
            whole(pair.shape),
            whole((width, width)),
            whole(vec.shape),
            whole(cot.shape),
            pl.BlockSpec((step, width), lambda i, s: (lax.rem(i + part, count), 0)),
            pl.BlockSpec((step, width), lambda i, s: (lax.rem(i + part, count), 0)),
        ],
        [
            whole((seq, width)),
            whole((seq, width)),
            whole((seq, 128)),
            pl.BlockSpec((seq, step), lambda i, s: (0, jnp.minimum(i, part - 1))),
            pl.BlockSpec((seq, step), lambda i, s: (0, jnp.maximum(i - part, 0))),
            pl.BlockSpec((seq, step), lambda i, s: (0, lax.rem(i + part, count))),
            whole((seq, width)),
            whole((seq, width)),
            whole((seq, 128)),
            whole((8, width)),
        ],
        shapes,
    )


def backward_kernel(last, outer_ref, start_ref, slope_ref, in_ref, back_ref, *refs):
    step = pl.program_id(0)
    if last:
        normal_ref, scale_ref, out_w_ref, vec_ref, two_ref, send_ref, keep_ref, total_ref, branch_ref, att_ref = refs
    else:
        send_ref, keep_ref, total_ref = refs
    grad_inner = (dot_nt(outer_ref[...], back_ref[...]) * slope_ref[...]).astype(BF)
    more = dot_nn(grad_inner, in_ref[...])

    @pl.when(step == 0)
    def _():
        send_ref[...] = grad_inner
        total_ref[...] = start_ref[...] + more

    @pl.when(step > 0)
    def _():
        keep_ref[...] = grad_inner
        total_ref[...] += more

    if last:

        @pl.when(step == pl.num_programs(0) - 1)
        def _():
            grad = total_ref[...]
            normal = normal_ref[...]
            seq = grad.shape[0]
            one = jnp.sum(grad * normal, axis=0, keepdims=True)
            two = jnp.sum(grad, axis=0, keepdims=True)
            lines = [one, two, two_ref[0:2, :], jnp.zeros((12, grad.shape[1]), F32)]
            branch_ref[seq:, :] = jnp.concatenate(lines, axis=0).astype(BF)
            grad_sum = norm_back(grad, normal, scale_ref[:, 0:1], vec_ref[0:1, :])
            total_ref[...] = grad_sum
            branch = grad_sum.astype(BF)
            branch_ref[:seq, :] = branch
            att_ref[...] = dot_nt(branch, out_w_ref[...]).astype(BF)


def backward(outer, start, slope, in_rows, back_rows, high, rest, after):
    seq, width = outer.shape
    units = in_rows.shape[0]
    step = units // 4
    chunk = lambda i: 2 * (1 - i) + high
    shapes = [jax.ShapeDtypeStruct((seq, step), BF)] * 2 + [jax.ShapeDtypeStruct((seq, width), F32)]
    if rest:
        shapes += [jax.ShapeDtypeStruct((seq + 16, width), BF), jax.ShapeDtypeStruct((seq, width), BF)]
    return run(
        functools.partial(backward_kernel, bool(rest)), "backward", 7, (),
        (outer, start, slope, in_rows, back_rows) + tuple(rest), (2,),
        [
            whole((seq, width)),
            whole((seq, width)),
            pl.BlockSpec((seq, step), lambda i: (0, chunk(i))),
            pl.BlockSpec((step, width), lambda i: (chunk(i), 0)),
            pl.BlockSpec((step, width), lambda i: (chunk(i), 0)),
        ]
        + [whole(r.shape) for r in rest],
        [whole(x.shape) for x in shapes],
        shapes,
        (),
        after,
    )


def unit_grad_kernel(own_ref, recv_ref, own_other, recv_other, out_ref):
    out_ref[...] = (dot_tn(own_ref[...], own_other[...]) + dot_tn(recv_ref[...], recv_other[...])).astype(BF)


def unit_grad(own, recv, own_other, recv_other, column, after):
    seq, width = own_other.shape
    step = 768
    shape = jax.ShapeDtypeStruct((step, width), BF)
    piece = pl.BlockSpec((seq, step), lambda i: (0, column))
    (out,), token = run(
        unit_grad_kernel, "unit_grad", 1.5, (), (own, recv, own_other, recv_other), (1,),
        [piece, piece, whole(own_other.shape), whole(recv_other.shape)], [whole(shape.shape)], [shape], (), after,
    )
    return out, token


def hot_columns(place, rows):
    return (iota((rows, place.shape[1]), 0) == place).astype(F32).astype(BF)


def move_kernel(order_ref, own_ref, recv_ref, own_out, recv_out):
    hot = hot_columns(order_ref[0:1, :], own_ref.shape[2])
    own_out[...] = dot_nn(own_ref[0], hot).astype(BF)
    recv_out[...] = dot_nn(recv_ref[0], hot).astype(BF)


def move(order, pair, pair_recv, after):
    _, seq, width = pair.shape
    shape = jax.ShapeDtypeStruct((seq, width), BF)
    part = pl.BlockSpec((1, seq, width), lambda i: (0, 0, 0))
    return run(
        move_kernel, "move", 1.5, (), (order, pair, pair_recv), (1,),
        [whole(order.shape), part, part], [whole(shape.shape)] * 2, [shape] * 2, (), after,
    )


def out_grad_kernel(spots_ref, branch_ref, branch_recv, att_ref, att_recv, low_ref, high_ref):
    seq, width = att_ref.shape[1:]
    rows = low_ref.shape[0]
    hot = hot_columns(spots_ref[0:1, :], width)
    moved = dot_nn(branch_ref[:seq, :], hot).astype(BF)
    moved_recv = dot_nn(branch_recv[:seq, :], hot).astype(BF)
    grad = (dot_tn(moved, att_ref[0]) + dot_tn(moved_recv, att_recv[0])).astype(BF)
    sums = branch_ref[seq:, :].astype(F32) + branch_recv[seq:, :].astype(F32)
    lines = jnp.concatenate([sums, jnp.zeros((112, width), F32)], axis=0).astype(BF)
    sums = jnp.transpose(dot_nn(lines, hot)).astype(BF)
    for i, out in enumerate((low_ref, high_ref)):
        out[:, :width] = grad[i * rows : (i + 1) * rows]
        out[:, width:] = sums[i * rows : (i + 1) * rows]


def out_grad(spots, branch, branch_recv, pair, pair_recv, after):
    _, seq, width = pair.shape
    shape = jax.ShapeDtypeStruct((width // 4, width + 128), BF)
    part = pl.BlockSpec((1, seq, width), lambda i: (1, 0, 0))
    return run(
        out_grad_kernel, "out_grad", 2, (), (spots, branch, branch_recv, pair, pair_recv), (1,),
        [whole(spots.shape), whole(branch.shape), whole(branch.shape), part, part],
        [whole(shape.shape)] * 2, [shape] * 2, (), after,
    )


def side_grad_kernel(moved_ref, moved_recv, gproj_ref, gproj_recv, out_low, out_high, low_ref, high_ref):
    half = moved_ref.shape[1] // 2
    rows = half // 2
    low_ref[:, 6 * half :] = out_low[...]
    high_ref[:, 6 * half :] = out_high[...]
    for c in range(3):
        grad = (dot_tn(moved_ref[...], gproj_ref[c]) + dot_tn(moved_recv[...], gproj_recv[c])).astype(BF)
        for k in range(2):
            at = (3 * k + c) * half
            low_ref[:, at : at + half] = grad[2 * k * rows : (2 * k + 1) * rows]
            high_ref[:, at : at + half] = grad[(2 * k + 1) * rows : (2 * k + 2) * rows]


def side_grad(*args, after):
    half = args[0].shape[1] // 2
    shapes = [jax.ShapeDtypeStruct((half // 2, 8 * half + 128), BF)] * 2
    return run(
        side_grad_kernel, "side_grad", 4, (), args, (1,),
        [whole(a.shape) for a in args], [whole(x.shape) for x in shapes], shapes, (), after,
    )


def swap_head(x):
    return lax.ppermute(x, "head", [(0, 1), (1, 0)])


def swap_dp(x, bit):
    return lax.ppermute(x, "dp", [(i, i ^ bit) for i in range(lax.axis_size("dp"))])


def swap_both(x, bits):
    count = lax.axis_size("dp")
    pairs = [(2 * i + h, 2 * (i ^ bits[h]) + h) for i in range(count) for h in range(2)]
    return lax.ppermute(x, ("dp", "head"), pairs)


def add_kernel(keep_low, keep_high, recv_low, recv_high, send, keep):
    send[...] = keep_high[...] + recv_high[...]
    keep[...] = keep_low[...] + recv_low[...]


def add_whole_kernel(keep_ref, recv_ref, send, keep):
    half = keep.shape[0]
    total = keep_ref[...].astype(F32) + recv_ref[...].astype(F32)
    send[...] = total[half:].astype(BF)
    keep[...] = total[:half].astype(BF)


def add_halves(keep, recv, after=()):
    half, width = recv.shape[0] // 2, recv.shape[1]
    shape = jax.ShapeDtypeStruct((half, width), BF)
    if half % 16 and half % 8 == 0:
        return run(
            add_whole_kernel, "add_halves", 1, (), (keep, recv), (1,), [whole(recv.shape)] * 2,
            [whole(shape.shape)] * 2, [shape] * 2, (), after,
        )
    if half % 16:
        total = keep + recv
        return (total[half:], total[:half]), None
    steps = 2 if half % 32 == 0 and half >= 384 else 1
    block = half // steps
    low = pl.BlockSpec((block, width), lambda i: (i, 0))
    high = pl.BlockSpec((block, width), lambda i: (i + steps, 0))
    return run(
        add_kernel, "add_halves", 1, (), (keep, keep, recv, recv), (steps,), [low, high, low, high],
        [low, low], [shape, shape], (), after,
    )


class Sum:
    def __init__(self, bits, send, low=None):
        self.bits, self.keep, self.done = bits, low, 0
        self.swap(send)

    def swap(self, send):
        k = self.done
        if k < 2:
            self.recv = swap_both(send, (self.bits[0], self.bits[1]) if k == 0 else (self.bits[1], self.bits[0]))
        else:
            self.recv = swap_dp(send, self.bits[k])
        self.done += 1

    def step(self, token):
        (send, self.keep), token_out = add_halves(self.keep, self.recv, (token,))
        self.swap(send)
        return token if token_out is None else token_out

    def result(self):
        return self.keep.astype(F32) + self.recv.astype(F32)


def reversed_bits(count):
    bits = count.bit_length() - 1
    return [sum(((i >> b) & 1) << (bits - 1 - b) for b in range(bits)) for i in range(count)]


def swap_low(i):
    return (i & ~3) | ((i & 1) << 1) | ((i >> 1) & 1)


def body(
    token_ids,
    lengths,
    embed_table,
    qkv_weight,
    out_weight,
    first_gain,
    first_bias,
    in_weight,
    back_weight,
    second_gain,
    term_vector,
    cotangent,
):
    dp = lax.axis_index("dp")
    head = lax.axis_index("head")
    owners = lax.axis_size("dp")
    bits = [1 << b for b in range(owners.bit_length() - 1)]
    device = dp * 2 + head
    seq = token_ids.shape[0]
    table_rows, half = embed_table.shape
    width = 2 * half
    units = back_weight.shape[0]
    cap = 4 * seq // owners
    slots = owners * cap

    ids = jnp.broadcast_to(token_ids.reshape(1, seq), (2 * owners, seq))
    ids = lax.all_to_all(ids, ("dp", "head"), split_axis=0, concat_axis=0, tiled=True)
    picked, asked, slot_row, slot_col = pick(jnp.stack([dp, head]), ids, embed_table, cap)
    got = lax.all_to_all(picked.reshape(owners, cap, half), "dp", split_axis=0, concat_axis=0, tiled=True)

    rev = reversed_bits(owners)
    ways = jnp.array([rev, [swap_low(r) for r in rev]], jnp.int32)
    keep_blocks, send_blocks = (ways[head] ^ dp) * 2 + head, (ways[1 - head] ^ dp) * 2 + 1 - head
    unit_order = jnp.concatenate([keep_blocks, send_blocks])
    back_rows = jnp.take(back_weight.reshape(2 * owners, -1, width), unit_order, axis=0, mode="clip").reshape(units, width)
    in_rows = jnp.take(in_weight.T.reshape(2 * owners, -1, width), unit_order, axis=0, mode="clip").reshape(units, width)
    weight = jnp.concatenate([qkv_weight, swap_head(qkv_weight)], axis=2)
    out_block = width // (2 * owners)
    inside = jnp.arange(out_block, dtype=jnp.int32)[None, :]
    lines = lambda start: (start[:, None] * out_block + inside).reshape(1, half)
    spots = lines(keep_blocks)
    order = jnp.concatenate([lines(keep_blocks - head), lines(keep_blocks - head + 1)], axis=1)
    vec = jnp.concatenate(
        [jnp.stack([first_gain, first_bias, second_gain, term_vector]), jnp.zeros((4, width), F32)], axis=0
    )
    asked_rows = asked[:owners].reshape(slots // 512, 512)
    cot = jnp.broadcast_to(cotangent.reshape(seq, 1), (seq, 128))
    place = jnp.stack([head, lengths[0]]).astype(jnp.int32)

    corner = in_rows[:8, :128] + back_rows[:8, :128] + weight[0, :8, :128]
    send, t = regather(slot_col, got.reshape(slots, half), 1, (corner, vec, cot, spots, order, asked_rows))
    own, _ = regather(slot_col, got.reshape(slots, half), 0, (t,))
    other = swap_head(send)
    (pair, proj, stat), _ = attend(place, own, other, weight)
    pair_recv = swap_head(pair)
    (low, normal, scale, active_send, active, slope, mixed, outer, weights, sums), t = forward(
        place, pair, out_weight, vec, cot, in_rows, back_rows
    )
    low_recv, outer_recv, active_recv = swap_head(low), swap_head(outer), swap_head(active_send)
    (moved, moved_recv), t = move(order, pair, pair_recv, (t,))
    (inner_send, inner_high, total), t = backward(outer, mixed, slope, in_rows, back_rows, 1, (), (t,))
    inner_recv = swap_head(inner_send)
    high, t = unit_grad(active, active_recv, outer, outer_recv, 1, (t,))
    back = Sum(bits, high)
    high, t = unit_grad(inner_high, inner_recv, low, low_recv, 0, (t,))
    ins = Sum(bits, high)
    (inner_send, inner_low, grad_sum, branch, grad_att), t = backward(
        outer, total, slope, in_rows, back_rows, 0, (normal, scale, out_weight, vec, sums), (t,)
    )
    inner_recv, branch_recv = swap_head(inner_send), swap_head(branch)
    (gproj_send, total), t = attend_back(place, proj, grad_att, stat, weight, grad_sum, False, (t,))
    gproj_recv = swap_head(gproj_send)
    back.keep, t = unit_grad(active, active_recv, outer, outer_recv, 0, (t,))
    t = back.step(t)
    ins.keep, t = unit_grad(inner_low, inner_recv, low, low_recv, 0, (t,))
    out_parts, t = out_grad(spots, branch, branch_recv, pair, pair_recv, (t,))
    (gproj, grad_own, grad_send), t = attend_back(place, proj, grad_att, stat, weight, total, True, (t,))
    grad_other = swap_head(grad_send)
    t = back.step(t)
    t = ins.step(t)
    (side_low, side_high), t = side_grad(moved, moved_recv, gproj, gproj_recv, *out_parts, after=(t,))
    side = Sum(bits, side_high, side_low)
    t = back.step(t)
    t = ins.step(t)
    (sent,), t = spread(slot_row, grad_own, grad_other, slots, (t,))
    arrived = lax.all_to_all(sent.reshape(owners, cap, half), "dp", split_axis=0, concat_axis=0, tiled=True)
    t = side.step(t)
    t = ins.step(t)
    t = side.step(t)
    (grad_table,), t = table_grad(asked_rows, arrived.reshape(slots, half), table_rows, (t,))
    while min(back.done, ins.done, side.done) < len(bits):
        for one in (side, ins, back):
            if one.done < len(bits):
                t = one.step(t)
    grad_back, grad_in, side = back.result(), ins.result(), side.result()
    grad_out, vectors = side[:, 6 * half : 8 * half], side[:, 8 * half :]
    grad_qkv = jnp.concatenate([side[:, : 3 * half], side[:, 3 * half : 6 * half]], axis=0)
    grad_qkv = grad_qkv.reshape(-1, 3, half).transpose(1, 0, 2)
    return (
        weights[:, 0],
        grad_table,
        grad_qkv,
        grad_out.T,
        grad_in.T,
        grad_back,
        vectors[:, 0],
        vectors[:, 1],
        vectors[:, 2],
        vectors[:, 3],
    )


def solution(mesh):
    in_specs = (
        P(("dp", "head")),
        P(("dp", "head")),
        P("dp", "head"),
        P(None, None, "head"),
        P(),
        P(),
        P(),
        P(),
        P(),
        P(),
        P(),
        P(("dp", "head")),
    )
    out_specs = (
        P(("dp", "head")),
        P("dp", "head"),
        P(None, "dp", "head"),
        P(None, ("dp", "head")),
        P(None, ("dp", "head")),
        P(("dp", "head"), None),
        P(("dp", "head")),
        P(("dp", "head")),
        P(("dp", "head")),
        P(("dp", "head")),
    )
    return jax.shard_map(body, mesh=mesh, in_specs=in_specs, out_specs=out_specs, check_vma=False)
```

```python
import functools

import jax
import jax.numpy as jnp
from jax import lax
from jax.experimental import pallas as pl
from jax.experimental.pallas import tpu as pltpu
from jax.sharding import PartitionSpec as P

HDIM = 64
LOG2E = 1.4426950408889634
BF = jnp.bfloat16
F32 = jnp.float32


def dot_nn(a, b):
    return lax.dot_general(a, b, (((1,), (0,)), ((), ())), preferred_element_type=F32)


def dot_nt(a, b):
    return lax.dot_general(a, b, (((1,), (1,)), ((), ())), preferred_element_type=F32)


def dot_tn(a, b):
    return lax.dot_general(a, b, (((0,), (0,)), ((), ())), preferred_element_type=F32)


def iota(shape, dim):
    return lax.broadcasted_iota(jnp.int32, shape, dim)


def params(mib):
    return pltpu.CompilerParams(vmem_limit_bytes=mib * 1024 * 1024)


def whole(shape):
    return pl.BlockSpec(shape, lambda *_: (0,) * len(shape))


def cost(micros):
    return pl.CostEstimate(flops=0, bytes_accessed=int(micros * 1e3), transcendentals=0)


ANY = pl.BlockSpec(memory_space=pl.ANY)


def run(kernel, name, micros, scalars, args, grid, in_specs, out_specs, shapes, scratch=(), after=(), mib=16):
    first, count = len(scalars) + len(args), len(after)

    def inner(*refs):
        refs = refs[:first] + refs[first + count :]
        spot = first + len(shapes)
        kernel(*refs[:spot], *refs[spot + 1 :])

    *outs, token = pl.pallas_call(
        inner,
        grid_spec=pltpu.PrefetchScalarGridSpec(
            num_scalar_prefetch=len(scalars),
            grid=grid,
            in_specs=list(in_specs) + [ANY] * count,
            out_specs=list(out_specs) + [ANY],
            scratch_shapes=list(scratch),
        ),
        out_shape=list(shapes) + [jax.ShapeDtypeStruct((8, 128), F32)],
        compiler_params=params(mib),
        cost_estimate=cost(micros),
        name=name,
    )(*scalars, *args, *after)
    return outs, token


def pick_kernel(place, ids_ref, table_ref, picked_ref, asked_ref, row_ref, col_ref, rank_s, away_s, hot_s):
    lines, seq = ids_ref.shape
    owners = lines // 2
    rows = table_ref.shape[0]
    cap = picked_ref.shape[0] // owners
    dp, head = place[0], place[1]
    away = ids_ref[...] - dp * rows
    mine = (away >= 0) & (away < rows)
    floor = iota((owners, seq), 0) * rows
    marks = []
    for core in range(2):
        own_ids = ids_ref[pl.ds(2 * dp + core, 1), :]
        marks.append((own_ids >= floor) & (own_ids < floor + rows))
    every = jnp.concatenate([m.astype(F32) for m in [mine] + marks], axis=0).astype(BF)
    upto = (iota((seq, seq), 0) <= iota((seq, seq), 1)).astype(F32).astype(BF)
    counts = dot_nn(every, upto)
    line, other = iota((lines, lines), 0), iota((lines, lines), 1)
    before = ((other == line - 1) & (line % 2 == 1)).astype(F32).astype(BF)
    ends = jnp.broadcast_to(counts[:lines, seq - 1 :], (lines, 128)).astype(BF)
    start = dot_nn(before, ends)[:, 0:1]
    rank_s[...] = (jnp.where(mine, counts[:lines] + start, 0.0) - 1.0).astype(jnp.int32)
    away_s[...] = away
    first, second = counts[lines : lines + owners], counts[lines + owners :]
    base = iota((owners, seq), 0).astype(F32) * cap - 1.0
    slots = [
        jnp.sum(jnp.where(marks[0], first + base, 0.0), axis=0, keepdims=True),
        jnp.sum(jnp.where(marks[1], second + first[:, seq - 1 :] + base, 0.0), axis=0, keepdims=True),
    ]
    own = jnp.where(head == 0, slots[0], slots[1])
    partner = jnp.where(head == 0, slots[1], slots[0])
    slot = jnp.concatenate([own, partner], axis=1)
    row_ref[...] = jnp.broadcast_to(slot, row_ref.shape)
    col_ref[...] = jnp.transpose(jnp.broadcast_to(slot, (128, 2 * seq)))
    group = hot_s.shape[0] // cap
    spots = iota((cap, seq), 0)
    lanes = iota((cap, 128), 1)

    def per_group(g, table_of):
        for i in range(group):
            j = g * group + i
            asked = 0
            for core in range(2):
                here = pl.ds(2 * j + core, 1)
                found = jnp.where(spots == rank_s[here, :], away_s[here, :], 0)
                asked = asked + jnp.sum(found, axis=1, keepdims=True)
            table_of = jnp.where(lanes == j, asked, table_of)
            hot_s[i * cap : (i + 1) * cap, :] = (iota((cap, rows), 1) == asked).astype(F32).astype(BF)
        size = group * cap
        picked_ref[pl.ds(pl.multiple_of(g * size, size), size), :] = dot_nn(hot_s[...], table_ref[...]).astype(BF)
        return table_of

    table_of = lax.fori_loop(0, owners // group, per_group, jnp.zeros((cap, 128), jnp.int32))
    asked_ref[...] = jnp.transpose(table_of.astype(F32))


def pick(place, ids, table, cap):
    lines, seq = ids.shape
    owners = lines // 2
    rows, half = table.shape
    group = min(owners, max(1, 512 // cap))
    shapes = (
        jax.ShapeDtypeStruct((owners * cap, half), BF),
        jax.ShapeDtypeStruct((128, cap), F32),
        jax.ShapeDtypeStruct((8, 2 * seq), F32),
        jax.ShapeDtypeStruct((2 * seq, 128), F32),
    )
    return run(
        pick_kernel, "pick", 9, (place,), (ids, table), (1,),
        [whole(ids.shape), whole(table.shape)],
        [whole(s.shape) for s in shapes],
        shapes,
        [pltpu.VMEM((lines, seq), jnp.int32)] * 2 + [pltpu.VMEM((group * cap, rows), BF)],
    )[0]


def regather_kernel(col_ref, got_ref, out_ref):
    slot = col_ref[:, 0:1].astype(jnp.int32)
    hot = (iota((out_ref.shape[0], got_ref.shape[0]), 1) == slot).astype(F32).astype(BF)
    out_ref[...] = dot_nn(hot, got_ref[...]).astype(BF)


def regather(col, got, part, after):
    half, width = col.shape[0] // 2, got.shape[1]
    shape = jax.ShapeDtypeStruct((half, width), BF)
    (out,), token = run(
        regather_kernel, "regather", 2, (), (col, got), (1,),
        [pl.BlockSpec((half, 128), lambda i: (part, 0)), whole(got.shape)], [whole(shape.shape)], [shape], (), after,
    )
    return out, token


def spread_kernel(row_ref, own_ref, other_ref, out_ref):
    half = own_ref.shape[0]
    step = out_ref.shape[0]
    base = pl.program_id(0) * step
    slot = row_ref[0:1, :].astype(jnp.int32)
    place = iota((step, half), 0) + base
    hot_own = (place == slot[:, :half]).astype(F32).astype(BF)
    hot_other = (place == slot[:, half:]).astype(F32).astype(BF)
    out_ref[...] = (dot_nn(hot_own, own_ref[...]) + dot_nn(hot_other, other_ref[...])).astype(BF)


def spread(row, own, other, slots, after):
    step = 512
    return run(
        spread_kernel, "spread", 3.7, (), (row, own, other), (slots // step,),
        [whole(row.shape), whole(own.shape), whole(other.shape)],
        [pl.BlockSpec((step, own.shape[1]), lambda i: (i, 0))],
        [jax.ShapeDtypeStruct((slots, own.shape[1]), BF)],
        (),
        after,
    )


def table_kernel(asked_ref, got_ref, out_ref):
    step = out_ref.shape[0]
    base = pl.program_id(0) * step
    total = jnp.zeros(out_ref.shape, F32)
    lines, width = asked_ref.shape
    for c in range(lines):
        asked = asked_ref[c : c + 1, :].astype(jnp.int32)
        hot = (iota((step, width), 0) + base == asked).astype(F32).astype(BF)
        total = total + dot_nn(hot, got_ref[c * width : (c + 1) * width, :])
    out_ref[...] = total


def table_grad(asked, got, rows, after):
    step = 640 if rows % 640 == 0 else rows
    return run(
        table_kernel, "table_grad", 5.5, (), (asked, got), (rows // step,),
        [whole(asked.shape), whole(got.shape)],
        [pl.BlockSpec((step, got.shape[1]), lambda i: (i, 0))],
        [jax.ShapeDtypeStruct((rows, got.shape[1]), F32)],
        (),
        after,
    )


SCALE = 0.125 * LOG2E


def head_views(key, query, length):
    lane = iota(query.shape, 1)
    dead = jnp.where(iota(key.shape, 0) < length, 0.0, -1e30).astype(BF)
    one, zero = jnp.ones_like(query), jnp.zeros_like(query)
    views = []
    for h in range(2):
        spare = HDIM if h == 0 else 0
        this = (lane < HDIM) if h == 0 else (lane >= HDIM)
        keys = jnp.where(lane == spare, dead, key)
        queries = jnp.where(this, query, jnp.where(lane == spare, one, zero))
        views.append((this, keys, queries))
    return views


def half_column(place, mine, half):
    return place[0] * half if mine else (1 - place[0]) * half


def attend_kernel(place, own_ref, other_ref, weight_ref, pair_ref, proj_ref, stat_ref):
    half = own_ref.shape[1]
    seq = own_ref.shape[0]

    @pl.when(place[0] == 0)
    def _():
        pair_ref[0, :, :half] = own_ref[...]
        pair_ref[0, :, half:] = other_ref[...]

    @pl.when(place[0] != 0)
    def _():
        pair_ref[0, :, :half] = other_ref[...]
        pair_ref[0, :, half:] = own_ref[...]

    for c in range(3):
        proj_ref[c] = dot_nn(pair_ref[0], weight_ref[c]).astype(BF)
    lane = iota((seq, 128), 1)
    pairs = 2 * half // 128

    def scores_of(p):
        here = slice(p * 128, (p + 1) * 128)
        views = head_views(proj_ref[1, :, here], proj_ref[0, :, here], place[1])
        return [dot_nt(queries, keys) for _, keys, queries in views]

    stat = jnp.zeros((seq, 128), F32)
    scores = scores_of(0)
    for p in range(pairs):
        later = scores_of(p + 1) if p + 1 < pairs else None
        value = proj_ref[2, :, p * 128 : (p + 1) * 128]
        parts = []
        for h in range(2):
            top = jnp.max(scores[h], axis=1, keepdims=True) * SCALE
            power = jnp.exp2(scores[h] * SCALE - top)
            total = jnp.sum(power, axis=1, keepdims=True)
            stat = jnp.where(lane == 2 * p + h, top + jnp.log2(total), stat)
            parts.append(dot_nn(power.astype(BF), value) * (1.0 / total))
        mine = p < pairs // 2
        column = half_column(place, mine, half) + (p if mine else p - pairs // 2) * 128
        spot = pl.ds(pl.multiple_of(column, 128), 128)
        pair_ref[1, :, spot] = jnp.where(lane < HDIM, parts[0], parts[1]).astype(BF)
        scores = later
    stat_ref[...] = stat


def attend(place, own, other, weight):
    seq, half = own.shape
    width = 2 * half
    shapes = (
        jax.ShapeDtypeStruct((2, seq, width), BF),
        jax.ShapeDtypeStruct((3, seq, width), BF),
        jax.ShapeDtypeStruct((seq, 128), F32),
    )
    args = (own, other, weight)
    return run(
        attend_kernel, "attend", 9, (place,), args, (1,),
        [whole(a.shape) for a in args], [whole(x.shape) for x in shapes], shapes, mib=32,
    )


def attend_back_kernel(mine, place, proj_ref, grad_ref, stat_ref, weight_ref, sum_ref, gproj_ref, *outs):
    seq, width = grad_ref.shape
    half = width // 2
    base = 0 if mine else half
    column = half_column(place, mine, half)
    lane = iota((seq, 128), 1)
    stat = stat_ref[...]
    for p in range(half // 128):
        here = slice(base + p * 128, base + (p + 1) * 128)
        query, key, value = proj_ref[0, :, here], proj_ref[1, :, here], proj_ref[2, :, here]
        grad = grad_ref[:, pl.ds(pl.multiple_of(column + p * 128, 128), 128)]
        query_t, grad_t = jnp.transpose(query), jnp.transpose(grad)
        grads_q, keys_t, values_t = [], [], []
        for h, (this, keys, queries) in enumerate(head_views(key, query, place[1])):
            rows = slice(h * HDIM, (h + 1) * HDIM)
            at = base // HDIM + 2 * p + h
            probs = jnp.exp2(dot_nt(queries, keys) * SCALE - stat[:, at : at + 1])
            grad_probs = dot_nt(jnp.where(this, grad, jnp.zeros_like(grad)), value)
            values_t.append(dot_nn(grad_t[rows], probs.astype(BF)))
            dots = jnp.sum(probs * grad_probs, axis=1, keepdims=True)
            grad_raw = (probs * (grad_probs - dots)).astype(BF)
            grads_q.append(dot_nn(grad_raw, key))
            keys_t.append(dot_nn(query_t[rows], grad_raw))
        here = slice(p * 128, (p + 1) * 128)
        gproj_ref[0, :, here] = (jnp.where(lane < HDIM, grads_q[0], grads_q[1]) * 0.125).astype(BF)
        gproj_ref[1, :, here] = jnp.transpose((jnp.concatenate(keys_t, axis=0) * 0.125).astype(BF))
        gproj_ref[2, :, here] = jnp.transpose(jnp.concatenate(values_t, axis=0).astype(BF))
    total = sum_ref[...]
    for c in range(3):
        total = total + dot_nt(gproj_ref[c], weight_ref[c, :, base : base + half])
    if not mine:
        outs[0][...] = total
        return
    own_ref, send_ref = outs
    low = total.astype(BF)

    @pl.when(place[0] == 0)
    def _():
        own_ref[...] = low[:, :half]
        send_ref[...] = low[:, half:]

    @pl.when(place[0] != 0)
    def _():
        own_ref[...] = low[:, half:]
        send_ref[...] = low[:, :half]


def attend_back(place, proj, grad, stat, weight, grad_sum, mine, after):
    seq, width = grad.shape
    half = width // 2
    shapes = [jax.ShapeDtypeStruct((3, seq, half), BF)]
    if mine:
        shapes += [jax.ShapeDtypeStruct((seq, half), BF)] * 2
    else:
        shapes += [jax.ShapeDtypeStruct((seq, width), F32)]
    args = (proj, grad, stat, weight, grad_sum)
    return run(
        functools.partial(attend_back_kernel, mine), "attend_back", 9, (place,), args, (1,),
        [whole(a.shape) for a in args], [whole(x.shape) for x in shapes], shapes, (), after, 32,
    )


def gelu_parts(x):
    t = 1.0 / (1.0 + (0.3275911 * 0.7071067811865476) * jnp.abs(x))
    bell = jnp.exp2(x * x * (-0.5 * LOG2E))
    poly = 0.127414796 + t * (-0.142248368 + t * (0.7107068705 + t * (-0.7265760135 + t * 0.5307027145)))
    tail = bell * (t * poly)
    below = jnp.where(x >= 0, 1.0 - tail, tail)
    return x * below, below + x * (bell * 0.3989422804014327)


def norm_parts(v):
    centre = v - jnp.mean(v, axis=-1, keepdims=True)
    spread_of = jnp.mean(centre * centre, axis=-1, keepdims=True)
    scale = lax.rsqrt(spread_of + 1e-12)
    return centre * scale, scale


def norm_back(grad, normal, scale, gain):
    e = grad * gain
    return scale * (e - jnp.mean(e, -1, keepdims=True) - normal * jnp.mean(e * normal, -1, keepdims=True))


def forward_kernel(
    place, pair_ref, out_w_ref, vec_ref, cot_ref, in_ref, back_ref,
    low_ref, normal_ref, scale_ref, send_ref, keep_ref, slope_ref, mixed_ref, outer_ref, weights_ref, sums_ref,
):
    seq = low_ref.shape[0]
    units = in_ref.shape[0]
    step = 768
    total = pair_ref[0].astype(F32) + dot_nn(pair_ref[1], out_w_ref[...])
    normal, scale = norm_parts(total)
    normed = normal * vec_ref[0:1, :] + vec_ref[1:2, :]
    normal_ref[...] = normal
    scale_ref[...] = jnp.broadcast_to(scale, scale_ref.shape)
    low_ref[...] = normed.astype(BF)
    mixed_ref[...] = normed
    inner = dot_nt(low_ref[...], in_ref[:step, :])
    for k in range(units // step):
        at = slice(k * step, (k + 1) * step)
        later = dot_nt(low_ref[...], in_ref[(k + 1) * step : (k + 2) * step, :]) if k + 1 < units // step else None
        active, slope = gelu_parts(inner)
        active = active.astype(BF)
        slope_ref[:, at] = slope
        if (k + 1) * step <= units // 2:
            keep_ref[:, at] = active
        else:
            send_ref[:, k * step - units // 2 : (k + 1) * step - units // 2] = active
        mixed_ref[...] += dot_nn(active, back_ref[at, :])
        inner = later
    normal, scale = norm_parts(mixed_ref[...])
    gain, term = vec_ref[2:3, :], vec_ref[3:4, :]
    final = normal * gain
    logit = jnp.sum(final * term, axis=-1, keepdims=True)
    live = (iota((seq, 1), 0) < place[1]).astype(F32)
    rest = jnp.exp(-jnp.abs(logit))
    weights = (jnp.maximum(logit, 0.0) + jnp.log1p(rest)) * live
    weights_ref[...] = jnp.broadcast_to(weights, weights_ref.shape)
    sigmoid = jnp.where(logit >= 0, 1.0, rest) / (1.0 + rest)
    grad_logit = cot_ref[:, 0:1] * live * sigmoid
    grad_final = grad_logit * term
    sums_ref[0:1, :] = jnp.sum(grad_final * normal, axis=0, keepdims=True)
    sums_ref[1:2, :] = jnp.sum(grad_logit * final, axis=0, keepdims=True)
    sums_ref[2:8, :] = jnp.zeros((6, sums_ref.shape[1]), F32)
    grad_mixed = norm_back(grad_final, normal, scale, gain)
    mixed_ref[...] = grad_mixed
    outer_ref[...] = grad_mixed.astype(BF)


def forward(place, pair, out_w, vec, cot, in_rows, back_rows):
    _, seq, width = pair.shape
    units = in_rows.shape[0]
    shapes = (
        jax.ShapeDtypeStruct((seq, width), BF),
        jax.ShapeDtypeStruct((seq, width), F32),
        jax.ShapeDtypeStruct((seq, 128), F32),
        jax.ShapeDtypeStruct((seq, units // 2), BF),
        jax.ShapeDtypeStruct((seq, units // 2), BF),
        jax.ShapeDtypeStruct((seq, units), F32),
        jax.ShapeDtypeStruct((seq, width), F32),
        jax.ShapeDtypeStruct((seq, width), BF),
        jax.ShapeDtypeStruct((seq, 128), F32),
        jax.ShapeDtypeStruct((8, width), F32),
    )
    args = (pair, out_w, vec, cot, in_rows, back_rows)
    return run(
        forward_kernel, "forward", 17, (place,), args, (1,),
        [whole(a.shape) for a in args], [whole(x.shape) for x in shapes], shapes, mib=24,
    )


def backward_kernel(last, outer_ref, start_ref, slope_ref, in_ref, back_ref, *refs):
    step = pl.program_id(0)
    if last:
        normal_ref, scale_ref, out_w_ref, vec_ref, two_ref, send_ref, keep_ref, total_ref, branch_ref, att_ref = refs
    else:
        send_ref, keep_ref, total_ref = refs
    grad_inner = (dot_nt(outer_ref[...], back_ref[...]) * slope_ref[...]).astype(BF)
    more = dot_nn(grad_inner, in_ref[...])

    @pl.when(step == 0)
    def _():
        send_ref[...] = grad_inner
        total_ref[...] = start_ref[...] + more

    @pl.when(step > 0)
    def _():
        keep_ref[...] = grad_inner
        total_ref[...] += more

    if last:

        @pl.when(step == pl.num_programs(0) - 1)
        def _():
            grad = total_ref[...]
            normal = normal_ref[...]
            seq = grad.shape[0]
            one = jnp.sum(grad * normal, axis=0, keepdims=True)
            two = jnp.sum(grad, axis=0, keepdims=True)
            lines = [one, two, two_ref[0:2, :], jnp.zeros((12, grad.shape[1]), F32)]
            branch_ref[seq:, :] = jnp.concatenate(lines, axis=0).astype(BF)
            grad_sum = norm_back(grad, normal, scale_ref[:, 0:1], vec_ref[0:1, :])
            total_ref[...] = grad_sum
            branch = grad_sum.astype(BF)
            branch_ref[:seq, :] = branch
            att_ref[...] = dot_nt(branch, out_w_ref[...]).astype(BF)


def backward(outer, start, slope, in_rows, back_rows, high, rest, after):
    seq, width = outer.shape
    units = in_rows.shape[0]
    step = units // 4
    chunk = lambda i: 2 * (1 - i) + high
    shapes = [jax.ShapeDtypeStruct((seq, step), BF)] * 2 + [jax.ShapeDtypeStruct((seq, width), F32)]
    if rest:
        shapes += [jax.ShapeDtypeStruct((seq + 16, width), BF), jax.ShapeDtypeStruct((seq, width), BF)]
    return run(
        functools.partial(backward_kernel, bool(rest)), "backward", 7, (),
        (outer, start, slope, in_rows, back_rows) + tuple(rest), (2,),
        [
            whole((seq, width)),
            whole((seq, width)),
            pl.BlockSpec((seq, step), lambda i: (0, chunk(i))),
            pl.BlockSpec((step, width), lambda i: (chunk(i), 0)),
            pl.BlockSpec((step, width), lambda i: (chunk(i), 0)),
        ]
        + [whole(r.shape) for r in rest],
        [whole(x.shape) for x in shapes],
        shapes,
        (),
        after,
    )


def unit_grad_kernel(own_ref, recv_ref, own_other, recv_other, out_ref):
    out_ref[...] = (dot_tn(own_ref[...], own_other[...]) + dot_tn(recv_ref[...], recv_other[...])).astype(BF)


def unit_grad(own, recv, own_other, recv_other, column, after):
    seq, width = own_other.shape
    step = 768
    shape = jax.ShapeDtypeStruct((step, width), BF)
    piece = pl.BlockSpec((seq, step), lambda i: (0, column))
    (out,), token = run(
        unit_grad_kernel, "unit_grad", 1.5, (), (own, recv, own_other, recv_other), (1,),
        [piece, piece, whole(own_other.shape), whole(recv_other.shape)], [whole(shape.shape)], [shape], (), after,
    )
    return out, token


def hot_columns(place, rows):
    return (iota((rows, place.shape[1]), 0) == place).astype(F32).astype(BF)


def move_kernel(order_ref, own_ref, recv_ref, own_out, recv_out):
    hot = hot_columns(order_ref[0:1, :], own_ref.shape[2])
    own_out[...] = dot_nn(own_ref[0], hot).astype(BF)
    recv_out[...] = dot_nn(recv_ref[0], hot).astype(BF)


def move(order, pair, pair_recv, after):
    _, seq, width = pair.shape
    shape = jax.ShapeDtypeStruct((seq, width), BF)
    part = pl.BlockSpec((1, seq, width), lambda i: (0, 0, 0))
    return run(
        move_kernel, "move", 1.5, (), (order, pair, pair_recv), (1,),
        [whole(order.shape), part, part], [whole(shape.shape)] * 2, [shape] * 2, (), after,
    )


def out_grad_kernel(spots_ref, branch_ref, branch_recv, att_ref, att_recv, low_ref, high_ref):
    seq, width = att_ref.shape[1:]
    rows = low_ref.shape[0]
    hot = hot_columns(spots_ref[0:1, :], width)
    moved = dot_nn(branch_ref[:seq, :], hot).astype(BF)
    moved_recv = dot_nn(branch_recv[:seq, :], hot).astype(BF)
    grad = (dot_tn(moved, att_ref[0]) + dot_tn(moved_recv, att_recv[0])).astype(BF)
    sums = branch_ref[seq:, :].astype(F32) + branch_recv[seq:, :].astype(F32)
    lines = jnp.concatenate([sums, jnp.zeros((112, width), F32)], axis=0).astype(BF)
    sums = jnp.transpose(dot_nn(lines, hot)).astype(BF)
    for i, out in enumerate((low_ref, high_ref)):
        out[:, :width] = grad[i * rows : (i + 1) * rows]
        out[:, width:] = sums[i * rows : (i + 1) * rows]


def out_grad(spots, branch, branch_recv, pair, pair_recv, after):
    _, seq, width = pair.shape
    shape = jax.ShapeDtypeStruct((width // 4, width + 128), BF)
    part = pl.BlockSpec((1, seq, width), lambda i: (1, 0, 0))
    return run(
        out_grad_kernel, "out_grad", 2, (), (spots, branch, branch_recv, pair, pair_recv), (1,),
        [whole(spots.shape), whole(branch.shape), whole(branch.shape), part, part],
        [whole(shape.shape)] * 2, [shape] * 2, (), after,
    )


def side_grad_kernel(moved_ref, moved_recv, gproj_ref, gproj_recv, out_low, out_high, low_ref, high_ref):
    half = moved_ref.shape[1] // 2
    rows = half // 2
    low_ref[:, 6 * half :] = out_low[...]
    high_ref[:, 6 * half :] = out_high[...]
    for c in range(3):
        grad = (dot_tn(moved_ref[...], gproj_ref[c]) + dot_tn(moved_recv[...], gproj_recv[c])).astype(BF)
        for k in range(2):
            at = (3 * k + c) * half
            low_ref[:, at : at + half] = grad[2 * k * rows : (2 * k + 1) * rows]
            high_ref[:, at : at + half] = grad[(2 * k + 1) * rows : (2 * k + 2) * rows]


def side_grad(*args, after):
    half = args[0].shape[1] // 2
    shapes = [jax.ShapeDtypeStruct((half // 2, 8 * half + 128), BF)] * 2
    return run(
        side_grad_kernel, "side_grad", 4, (), args, (1,),
        [whole(a.shape) for a in args], [whole(x.shape) for x in shapes], shapes, (), after,
    )


def swap_head(x):
    return lax.ppermute(x, "head", [(0, 1), (1, 0)])


def swap_dp(x, bit):
    return lax.ppermute(x, "dp", [(i, i ^ bit) for i in range(lax.axis_size("dp"))])


def swap_both(x, bits):
    count = lax.axis_size("dp")
    pairs = [(2 * i + h, 2 * (i ^ bits[h]) + h) for i in range(count) for h in range(2)]
    return lax.ppermute(x, ("dp", "head"), pairs)


def add_kernel(keep_low, keep_high, recv_low, recv_high, send, keep):
    send[...] = keep_high[...] + recv_high[...]
    keep[...] = keep_low[...] + recv_low[...]


def add_whole_kernel(keep_ref, recv_ref, send, keep):
    half = keep.shape[0]
    total = keep_ref[...].astype(F32) + recv_ref[...].astype(F32)
    send[...] = total[half:].astype(BF)
    keep[...] = total[:half].astype(BF)


def add_halves(keep, recv, after=()):
    half, width = recv.shape[0] // 2, recv.shape[1]
    shape = jax.ShapeDtypeStruct((half, width), BF)
    if half % 16 and half % 8 == 0:
        return run(
            add_whole_kernel, "add_halves", 1, (), (keep, recv), (1,), [whole(recv.shape)] * 2,
            [whole(shape.shape)] * 2, [shape] * 2, (), after,
        )
    if half % 16:
        total = keep + recv
        return (total[half:], total[:half]), None
    steps = 2 if half % 32 == 0 and half >= 384 else 1
    block = half // steps
    low = pl.BlockSpec((block, width), lambda i: (i, 0))
    high = pl.BlockSpec((block, width), lambda i: (i + steps, 0))
    return run(
        add_kernel, "add_halves", 1, (), (keep, keep, recv, recv), (steps,), [low, high, low, high],
        [low, low], [shape, shape], (), after,
    )


class Sum:
    def __init__(self, bits, send, low=None):
        self.bits, self.keep, self.done = bits, low, 0
        self.swap(send)

    def swap(self, send):
        k = self.done
        if k < 2:
            self.recv = swap_both(send, (self.bits[0], self.bits[1]) if k == 0 else (self.bits[1], self.bits[0]))
        else:
            self.recv = swap_dp(send, self.bits[k])
        self.done += 1

    def step(self, token):
        (send, self.keep), token_out = add_halves(self.keep, self.recv, (token,))
        self.swap(send)
        return token if token_out is None else token_out

    def result(self):
        return self.keep.astype(F32) + self.recv.astype(F32)


def reversed_bits(count):
    bits = count.bit_length() - 1
    return [sum(((i >> b) & 1) << (bits - 1 - b) for b in range(bits)) for i in range(count)]


def swap_low(i):
    return (i & ~3) | ((i & 1) << 1) | ((i >> 1) & 1)


def body(
    token_ids,
    lengths,
    embed_table,
    qkv_weight,
    out_weight,
    first_gain,
    first_bias,
    in_weight,
    back_weight,
    second_gain,
    term_vector,
    cotangent,
):
    dp = lax.axis_index("dp")
    head = lax.axis_index("head")
    owners = lax.axis_size("dp")
    bits = [1 << b for b in range(owners.bit_length() - 1)]
    device = dp * 2 + head
    seq = token_ids.shape[0]
    table_rows, half = embed_table.shape
    width = 2 * half
    units = back_weight.shape[0]
    cap = 4 * seq // owners
    slots = owners * cap

    ids = jnp.broadcast_to(token_ids.reshape(1, seq), (2 * owners, seq))
    ids = lax.all_to_all(ids, ("dp", "head"), split_axis=0, concat_axis=0, tiled=True)
    picked, asked, slot_row, slot_col = pick(jnp.stack([dp, head]), ids, embed_table, cap)
    got = lax.all_to_all(picked.reshape(owners, cap, half), "dp", split_axis=0, concat_axis=0, tiled=True)

    rev = reversed_bits(owners)
    ways = jnp.array([rev, [swap_low(r) for r in rev]], jnp.int32)
    keep_blocks, send_blocks = (ways[head] ^ dp) * 2 + head, (ways[1 - head] ^ dp) * 2 + 1 - head
    unit_order = jnp.concatenate([keep_blocks, send_blocks])
    back_rows = jnp.take(back_weight.reshape(2 * owners, -1, width), unit_order, axis=0, mode="clip").reshape(units, width)
    in_rows = jnp.take(in_weight.T.reshape(2 * owners, -1, width), unit_order, axis=0, mode="clip").reshape(units, width)
    weight = jnp.concatenate([qkv_weight, swap_head(qkv_weight)], axis=2)
    out_block = width // (2 * owners)
    inside = jnp.arange(out_block, dtype=jnp.int32)[None, :]
    lines = lambda start: (start[:, None] * out_block + inside).reshape(1, half)
    spots = lines(keep_blocks)
    order = jnp.concatenate([lines(keep_blocks - head), lines(keep_blocks - head + 1)], axis=1)
    vec = jnp.concatenate(
        [jnp.stack([first_gain, first_bias, second_gain, term_vector]), jnp.zeros((4, width), F32)], axis=0
    )
    asked_rows = asked[:owners].reshape(slots // 512, 512)
    cot = jnp.broadcast_to(cotangent.reshape(seq, 1), (seq, 128))
    place = jnp.stack([head, lengths[0]]).astype(jnp.int32)

    corner = in_rows[:8, :128] + back_rows[:8, :128] + weight[0, :8, :128]
    send, t = regather(slot_col, got.reshape(slots, half), 1, (corner, vec, cot, spots, order, asked_rows))
    own, _ = regather(slot_col, got.reshape(slots, half), 0, (t,))
    other = swap_head(send)
    (pair, proj, stat), _ = attend(place, own, other, weight)
    pair_recv = swap_head(pair)
    (low, normal, scale, active_send, active, slope, mixed, outer, weights, sums), t = forward(
        place, pair, out_weight, vec, cot, in_rows, back_rows
    )
    low_recv, outer_recv, active_recv = swap_head(low), swap_head(outer), swap_head(active_send)
    (inner_send, inner_high, total), t = backward(outer, mixed, slope, in_rows, back_rows, 1, (), (t,))
    inner_recv = swap_head(inner_send)
    (moved, moved_recv), t = move(order, pair, pair_recv, (t,))
    high, t = unit_grad(active, active_recv, outer, outer_recv, 1, (t,))
    back = Sum(bits, high)
    high, t = unit_grad(inner_high, inner_recv, low, low_recv, 0, (t,))
    ins = Sum(bits, high)
    (inner_send, inner_low, grad_sum, branch, grad_att), t = backward(
        outer, total, slope, in_rows, back_rows, 0, (normal, scale, out_weight, vec, sums), (t,)
    )
    inner_recv, branch_recv = swap_head(inner_send), swap_head(branch)
    (gproj_send, total), t = attend_back(place, proj, grad_att, stat, weight, grad_sum, False, (t,))
    gproj_recv = swap_head(gproj_send)
    back.keep, t = unit_grad(active, active_recv, outer, outer_recv, 0, (t,))
    t = back.step(t)
    ins.keep, t = unit_grad(inner_low, inner_recv, low, low_recv, 0, (t,))
    out_parts, t = out_grad(spots, branch, branch_recv, pair, pair_recv, (t,))
    (gproj, grad_own, grad_send), t = attend_back(place, proj, grad_att, stat, weight, total, True, (t,))
    grad_other = swap_head(grad_send)
    t = back.step(t)
    t = ins.step(t)
    (side_low, side_high), t = side_grad(moved, moved_recv, gproj, gproj_recv, *out_parts, after=(t,))
    side = Sum(bits, side_high, side_low)
    t = back.step(t)
    t = ins.step(t)
    (sent,), t = spread(slot_row, grad_own, grad_other, slots, (t,))
    arrived = lax.all_to_all(sent.reshape(owners, cap, half), "dp", split_axis=0, concat_axis=0, tiled=True)
    t = ins.step(t)
    t = side.step(t)
    t = side.step(t)
    (grad_table,), t = table_grad(asked_rows, arrived.reshape(slots, half), table_rows, (t,))
    while min(back.done, ins.done, side.done) < len(bits):
        for one in (side, ins, back):
            if one.done < len(bits):
                t = one.step(t)
    grad_back, grad_in, side = back.result(), ins.result(), side.result()
    grad_out, vectors = side[:, 6 * half : 8 * half], side[:, 8 * half :]
    grad_qkv = jnp.concatenate([side[:, : 3 * half], side[:, 3 * half : 6 * half]], axis=0)
    grad_qkv = grad_qkv.reshape(-1, 3, half).transpose(1, 0, 2)
    return (
        weights[:, 0],
        grad_table,
        grad_qkv,
        grad_out.T,
        grad_in.T,
        grad_back,
        vectors[:, 0],
        vectors[:, 1],
        vectors[:, 2],
        vectors[:, 3],
    )


def solution(mesh):
    in_specs = (
        P(("dp", "head")),
        P(("dp", "head")),
        P("dp", "head"),
        P(None, None, "head"),
        P(),
        P(),
        P(),
        P(),
        P(),
        P(),
        P(),
        P(("dp", "head")),
    )
    out_specs = (
        P(("dp", "head")),
        P("dp", "head"),
        P(None, "dp", "head"),
        P(None, ("dp", "head")),
        P(None, ("dp", "head")),
        P(("dp", "head"), None),
        P(("dp", "head")),
        P(("dp", "head")),
        P(("dp", "head")),
        P(("dp", "head")),
    )
    return jax.shard_map(body, mesh=mesh, in_specs=in_specs, out_specs=out_specs, check_vma=False)
```

```python
import functools

import jax
import jax.numpy as jnp
from jax import lax
from jax.experimental import pallas as pl
from jax.experimental.pallas import tpu as pltpu
from jax.sharding import PartitionSpec as P

HDIM = 64
LOG2E = 1.4426950408889634
BF = jnp.bfloat16
F32 = jnp.float32


def dot_nn(a, b):
    return lax.dot_general(a, b, (((1,), (0,)), ((), ())), preferred_element_type=F32)


def dot_nt(a, b):
    return lax.dot_general(a, b, (((1,), (1,)), ((), ())), preferred_element_type=F32)


def dot_tn(a, b):
    return lax.dot_general(a, b, (((0,), (0,)), ((), ())), preferred_element_type=F32)


def iota(shape, dim):
    return lax.broadcasted_iota(jnp.int32, shape, dim)


def params(mib):
    return pltpu.CompilerParams(vmem_limit_bytes=mib * 1024 * 1024)


def whole(shape):
    return pl.BlockSpec(shape, lambda *_: (0,) * len(shape))


def cost(micros):
    return pl.CostEstimate(flops=0, bytes_accessed=int(micros * 1e3), transcendentals=0)


ANY = pl.BlockSpec(memory_space=pl.ANY)


def run(kernel, name, micros, scalars, args, grid, in_specs, out_specs, shapes, scratch=(), after=(), mib=16):
    first, count = len(scalars) + len(args), len(after)

    def inner(*refs):
        refs = refs[:first] + refs[first + count :]
        spot = first + len(shapes)
        kernel(*refs[:spot], *refs[spot + 1 :])

    *outs, token = pl.pallas_call(
        inner,
        grid_spec=pltpu.PrefetchScalarGridSpec(
            num_scalar_prefetch=len(scalars),
            grid=grid,
            in_specs=list(in_specs) + [ANY] * count,
            out_specs=list(out_specs) + [ANY],
            scratch_shapes=list(scratch),
        ),
        out_shape=list(shapes) + [jax.ShapeDtypeStruct((8, 128), F32)],
        compiler_params=params(mib),
        cost_estimate=cost(micros),
        name=name,
    )(*scalars, *args, *after)
    return outs, token


def pick_kernel(place, ids_ref, table_ref, picked_ref, asked_ref, row_ref, col_ref, rank_s, away_s, hot_s):
    lines, seq = ids_ref.shape
    owners = lines // 2
    rows = table_ref.shape[0]
    cap = picked_ref.shape[0] // owners
    dp, head = place[0], place[1]
    away = ids_ref[...] - dp * rows
    mine = (away >= 0) & (away < rows)
    floor = iota((owners, seq), 0) * rows
    marks = []
    for core in range(2):
        own_ids = ids_ref[pl.ds(2 * dp + core, 1), :]
        marks.append((own_ids >= floor) & (own_ids < floor + rows))
    every = jnp.concatenate([m.astype(F32) for m in [mine] + marks], axis=0).astype(BF)
    upto = (iota((seq, seq), 0) <= iota((seq, seq), 1)).astype(F32).astype(BF)
    counts = dot_nn(every, upto)
    line, other = iota((lines, lines), 0), iota((lines, lines), 1)
    before = ((other == line - 1) & (line % 2 == 1)).astype(F32).astype(BF)
    ends = jnp.broadcast_to(counts[:lines, seq - 1 :], (lines, 128)).astype(BF)
    start = dot_nn(before, ends)[:, 0:1]
    rank_s[...] = (jnp.where(mine, counts[:lines] + start, 0.0) - 1.0).astype(jnp.int32)
    away_s[...] = away
    first, second = counts[lines : lines + owners], counts[lines + owners :]
    base = iota((owners, seq), 0).astype(F32) * cap - 1.0
    slots = [
        jnp.sum(jnp.where(marks[0], first + base, 0.0), axis=0, keepdims=True),
        jnp.sum(jnp.where(marks[1], second + first[:, seq - 1 :] + base, 0.0), axis=0, keepdims=True),
    ]
    own = jnp.where(head == 0, slots[0], slots[1])
    partner = jnp.where(head == 0, slots[1], slots[0])
    slot = jnp.concatenate([own, partner], axis=1)
    row_ref[...] = jnp.broadcast_to(slot, row_ref.shape)
    col_ref[...] = jnp.transpose(jnp.broadcast_to(slot, (128, 2 * seq)))
    group = hot_s.shape[0] // cap
    spots = iota((cap, seq), 0)
    lanes = iota((cap, 128), 1)

    def per_group(g, table_of):
        for i in range(group):
            j = g * group + i
            asked = 0
            for core in range(2):
                here = pl.ds(2 * j + core, 1)
                found = jnp.where(spots == rank_s[here, :], away_s[here, :], 0)
                asked = asked + jnp.sum(found, axis=1, keepdims=True)
            table_of = jnp.where(lanes == j, asked, table_of)
            hot_s[i * cap : (i + 1) * cap, :] = (iota((cap, rows), 1) == asked).astype(F32).astype(BF)
        size = group * cap
        picked_ref[pl.ds(pl.multiple_of(g * size, size), size), :] = dot_nn(hot_s[...], table_ref[...]).astype(BF)
        return table_of

    table_of = lax.fori_loop(0, owners // group, per_group, jnp.zeros((cap, 128), jnp.int32))
    asked_ref[...] = jnp.transpose(table_of.astype(F32))


def pick(place, ids, table, cap):
    lines, seq = ids.shape
    owners = lines // 2
    rows, half = table.shape
    group = min(owners, max(1, 512 // cap))
    shapes = (
        jax.ShapeDtypeStruct((owners * cap, half), BF),
        jax.ShapeDtypeStruct((128, cap), F32),
        jax.ShapeDtypeStruct((8, 2 * seq), F32),
        jax.ShapeDtypeStruct((2 * seq, 128), F32),
    )
    return run(
        pick_kernel, "pick", 9, (place,), (ids, table), (1,),
        [whole(ids.shape), whole(table.shape)],
        [whole(s.shape) for s in shapes],
        shapes,
        [pltpu.VMEM((lines, seq), jnp.int32)] * 2 + [pltpu.VMEM((group * cap, rows), BF)],
    )[0]


def regather_kernel(col_ref, got_ref, out_ref):
    slot = col_ref[:, 0:1].astype(jnp.int32)
    hot = (iota((out_ref.shape[0], got_ref.shape[0]), 1) == slot).astype(F32).astype(BF)
    out_ref[...] = dot_nn(hot, got_ref[...]).astype(BF)


def regather(col, got, part, after):
    half, width = col.shape[0] // 2, got.shape[1]
    shape = jax.ShapeDtypeStruct((half, width), BF)
    (out,), token = run(
        regather_kernel, "regather", 2, (), (col, got), (1,),
        [pl.BlockSpec((half, 128), lambda i: (part, 0)), whole(got.shape)], [whole(shape.shape)], [shape], (), after,
    )
    return out, token


def spread_kernel(row_ref, own_ref, other_ref, out_ref):
    half = own_ref.shape[0]
    step = out_ref.shape[0]
    base = pl.program_id(0) * step
    slot = row_ref[0:1, :].astype(jnp.int32)
    place = iota((step, half), 0) + base
    hot_own = (place == slot[:, :half]).astype(F32).astype(BF)
    hot_other = (place == slot[:, half:]).astype(F32).astype(BF)
    out_ref[...] = (dot_nn(hot_own, own_ref[...]) + dot_nn(hot_other, other_ref[...])).astype(BF)


def spread(row, own, other, slots, after):
    step = 512
    return run(
        spread_kernel, "spread", 3.7, (), (row, own, other), (slots // step,),
        [whole(row.shape), whole(own.shape), whole(other.shape)],
        [pl.BlockSpec((step, own.shape[1]), lambda i: (i, 0))],
        [jax.ShapeDtypeStruct((slots, own.shape[1]), BF)],
        (),
        after,
    )


def table_kernel(asked_ref, got_ref, out_ref):
    step = out_ref.shape[0]
    base = pl.program_id(0) * step
    total = jnp.zeros(out_ref.shape, F32)
    lines, width = asked_ref.shape
    for c in range(lines):
        asked = asked_ref[c : c + 1, :].astype(jnp.int32)
        hot = (iota((step, width), 0) + base == asked).astype(F32).astype(BF)
        total = total + dot_nn(hot, got_ref[c * width : (c + 1) * width, :])
    out_ref[...] = total


def table_grad(asked, got, rows, after):
    step = 640 if rows % 640 == 0 else rows
    return run(
        table_kernel, "table_grad", 5.5, (), (asked, got), (rows // step,),
        [whole(asked.shape), whole(got.shape)],
        [pl.BlockSpec((step, got.shape[1]), lambda i: (i, 0))],
        [jax.ShapeDtypeStruct((rows, got.shape[1]), F32)],
        (),
        after,
    )


SCALE = 0.125 * LOG2E


def head_views(key, query, length):
    lane = iota(query.shape, 1)
    dead = jnp.where(iota(key.shape, 0) < length, 0.0, -1e30).astype(BF)
    one, zero = jnp.ones_like(query), jnp.zeros_like(query)
    views = []
    for h in range(2):
        spare = HDIM if h == 0 else 0
        this = (lane < HDIM) if h == 0 else (lane >= HDIM)
        keys = jnp.where(lane == spare, dead, key)
        queries = jnp.where(this, query, jnp.where(lane == spare, one, zero))
        views.append((this, keys, queries))
    return views


def half_column(place, mine, half):
    return place[0] * half if mine else (1 - place[0]) * half


def attend_kernel(place, own_ref, other_ref, weight_ref, pair_ref, proj_ref, stat_ref):
    half = own_ref.shape[1]
    seq = own_ref.shape[0]

    @pl.when(place[0] == 0)
    def _():
        pair_ref[0, :, :half] = own_ref[...]
        pair_ref[0, :, half:] = other_ref[...]

    @pl.when(place[0] != 0)
    def _():
        pair_ref[0, :, :half] = other_ref[...]
        pair_ref[0, :, half:] = own_ref[...]

    for c in range(3):
        proj_ref[c] = dot_nn(pair_ref[0], weight_ref[c]).astype(BF)
    lane = iota((seq, 128), 1)
    pairs = 2 * half // 128

    def scores_of(p):
        here = slice(p * 128, (p + 1) * 128)
        views = head_views(proj_ref[1, :, here], proj_ref[0, :, here], place[1])
        return [dot_nt(queries, keys) for _, keys, queries in views]

    stat = jnp.zeros((seq, 128), F32)
    scores = scores_of(0)
    for p in range(pairs):
        later = scores_of(p + 1) if p + 1 < pairs else None
        value = proj_ref[2, :, p * 128 : (p + 1) * 128]
        parts = []
        for h in range(2):
            top = jnp.max(scores[h], axis=1, keepdims=True) * SCALE
            power = jnp.exp2(scores[h] * SCALE - top)
            total = jnp.sum(power, axis=1, keepdims=True)
            stat = jnp.where(lane == 2 * p + h, top + jnp.log2(total), stat)
            parts.append(dot_nn(power.astype(BF), value) * (1.0 / total))
        mine = p < pairs // 2
        column = half_column(place, mine, half) + (p if mine else p - pairs // 2) * 128
        spot = pl.ds(pl.multiple_of(column, 128), 128)
        pair_ref[1, :, spot] = jnp.where(lane < HDIM, parts[0], parts[1]).astype(BF)
        scores = later
    stat_ref[...] = stat


def attend(place, own, other, weight):
    seq, half = own.shape
    width = 2 * half
    shapes = (
        jax.ShapeDtypeStruct((2, seq, width), BF),
        jax.ShapeDtypeStruct((3, seq, width), BF),
        jax.ShapeDtypeStruct((seq, 128), F32),
    )
    args = (own, other, weight)
    return run(
        attend_kernel, "attend", 9, (place,), args, (1,),
        [whole(a.shape) for a in args], [whole(x.shape) for x in shapes], shapes, mib=32,
    )


def attend_back_kernel(mine, place, proj_ref, grad_ref, stat_ref, weight_ref, sum_ref, gproj_ref, *outs):
    seq, width = grad_ref.shape
    half = width // 2
    base = 0 if mine else half
    column = half_column(place, mine, half)
    lane = iota((seq, 128), 1)
    stat = stat_ref[...]
    for p in range(half // 128):
        here = slice(base + p * 128, base + (p + 1) * 128)
        query, key, value = proj_ref[0, :, here], proj_ref[1, :, here], proj_ref[2, :, here]
        grad = grad_ref[:, pl.ds(pl.multiple_of(column + p * 128, 128), 128)]
        query_t, grad_t = jnp.transpose(query), jnp.transpose(grad)
        grads_q, keys_t, values_t = [], [], []
        for h, (this, keys, queries) in enumerate(head_views(key, query, place[1])):
            rows = slice(h * HDIM, (h + 1) * HDIM)
            at = base // HDIM + 2 * p + h
            probs = jnp.exp2(dot_nt(queries, keys) * SCALE - stat[:, at : at + 1])
            grad_probs = dot_nt(jnp.where(this, grad, jnp.zeros_like(grad)), value)
            values_t.append(dot_nn(grad_t[rows], probs.astype(BF)))
            dots = jnp.sum(probs * grad_probs, axis=1, keepdims=True)
            grad_raw = (probs * (grad_probs - dots)).astype(BF)
            grads_q.append(dot_nn(grad_raw, key))
            keys_t.append(dot_nn(query_t[rows], grad_raw))
        here = slice(p * 128, (p + 1) * 128)
        gproj_ref[0, :, here] = (jnp.where(lane < HDIM, grads_q[0], grads_q[1]) * 0.125).astype(BF)
        gproj_ref[1, :, here] = jnp.transpose((jnp.concatenate(keys_t, axis=0) * 0.125).astype(BF))
        gproj_ref[2, :, here] = jnp.transpose(jnp.concatenate(values_t, axis=0).astype(BF))
    total = sum_ref[...]
    for c in range(3):
        total = total + dot_nt(gproj_ref[c], weight_ref[c, :, base : base + half])
    if not mine:
        outs[0][...] = total
        return
    own_ref, send_ref = outs
    low = total.astype(BF)

    @pl.when(place[0] == 0)
    def _():
        own_ref[...] = low[:, :half]
        send_ref[...] = low[:, half:]

    @pl.when(place[0] != 0)
    def _():
        own_ref[...] = low[:, half:]
        send_ref[...] = low[:, :half]


def attend_back(place, proj, grad, stat, weight, grad_sum, mine, after):
    seq, width = grad.shape
    half = width // 2
    shapes = [jax.ShapeDtypeStruct((3, seq, half), BF)]
    if mine:
        shapes += [jax.ShapeDtypeStruct((seq, half), BF)] * 2
    else:
        shapes += [jax.ShapeDtypeStruct((seq, width), F32)]
    args = (proj, grad, stat, weight, grad_sum)
    return run(
        functools.partial(attend_back_kernel, mine), "attend_back", 9, (place,), args, (1,),
        [whole(a.shape) for a in args], [whole(x.shape) for x in shapes], shapes, (), after, 32,
    )


def gelu_parts(x):
    t = 1.0 / (1.0 + (0.3275911 * 0.7071067811865476) * jnp.abs(x))
    bell = jnp.exp2(x * x * (-0.5 * LOG2E))
    poly = 0.127414796 + t * (-0.142248368 + t * (0.7107068705 + t * (-0.7265760135 + t * 0.5307027145)))
    tail = bell * (t * poly)
    below = jnp.where(x >= 0, 1.0 - tail, tail)
    return x * below, below + x * (bell * 0.3989422804014327)


def norm_parts(v):
    centre = v - jnp.mean(v, axis=-1, keepdims=True)
    spread_of = jnp.mean(centre * centre, axis=-1, keepdims=True)
    scale = lax.rsqrt(spread_of + 1e-12)
    return centre * scale, scale


def norm_back(grad, normal, scale, gain):
    e = grad * gain
    return scale * (e - jnp.mean(e, -1, keepdims=True) - normal * jnp.mean(e * normal, -1, keepdims=True))


def forward_kernel(
    place, pair_ref, out_w_ref, vec_ref, cot_ref, in_ref, back_ref,
    low_ref, normal_ref, scale_ref, send_ref, keep_ref, slope_ref, mixed_ref, outer_ref, weights_ref, sums_ref,
):
    seq = low_ref.shape[0]
    units = in_ref.shape[0]
    step = 768
    total = pair_ref[0].astype(F32) + dot_nn(pair_ref[1], out_w_ref[...])
    normal, scale = norm_parts(total)
    normed = normal * vec_ref[0:1, :] + vec_ref[1:2, :]
    normal_ref[...] = normal
    scale_ref[...] = jnp.broadcast_to(scale, scale_ref.shape)
    low_ref[...] = normed.astype(BF)
    mixed_ref[...] = normed
    inner = dot_nt(low_ref[...], in_ref[:step, :])
    for k in range(units // step):
        at = slice(k * step, (k + 1) * step)
        later = dot_nt(low_ref[...], in_ref[(k + 1) * step : (k + 2) * step, :]) if k + 1 < units // step else None
        active, slope = gelu_parts(inner)
        active = active.astype(BF)
        slope_ref[:, at] = slope
        if (k + 1) * step <= units // 2:
            keep_ref[:, at] = active
        else:
            send_ref[:, k * step - units // 2 : (k + 1) * step - units // 2] = active
        mixed_ref[...] += dot_nn(active, back_ref[at, :])
        inner = later
    normal, scale = norm_parts(mixed_ref[...])
    gain, term = vec_ref[2:3, :], vec_ref[3:4, :]
    final = normal * gain
    logit = jnp.sum(final * term, axis=-1, keepdims=True)
    live = (iota((seq, 1), 0) < place[1]).astype(F32)
    rest = jnp.exp(-jnp.abs(logit))
    weights = (jnp.maximum(logit, 0.0) + jnp.log1p(rest)) * live
    weights_ref[...] = jnp.broadcast_to(weights, weights_ref.shape)
    sigmoid = jnp.where(logit >= 0, 1.0, rest) / (1.0 + rest)
    grad_logit = cot_ref[:, 0:1] * live * sigmoid
    grad_final = grad_logit * term
    sums_ref[0:1, :] = jnp.sum(grad_final * normal, axis=0, keepdims=True)
    sums_ref[1:2, :] = jnp.sum(grad_logit * final, axis=0, keepdims=True)
    sums_ref[2:8, :] = jnp.zeros((6, sums_ref.shape[1]), F32)
    grad_mixed = norm_back(grad_final, normal, scale, gain)
    mixed_ref[...] = grad_mixed
    outer_ref[...] = grad_mixed.astype(BF)


def forward(place, pair, out_w, vec, cot, in_rows, back_rows):
    _, seq, width = pair.shape
    units = in_rows.shape[0]
    shapes = (
        jax.ShapeDtypeStruct((seq, width), BF),
        jax.ShapeDtypeStruct((seq, width), F32),
        jax.ShapeDtypeStruct((seq, 128), F32),
        jax.ShapeDtypeStruct((seq, units // 2), BF),
        jax.ShapeDtypeStruct((seq, units // 2), BF),
        jax.ShapeDtypeStruct((seq, units), F32),
        jax.ShapeDtypeStruct((seq, width), F32),
        jax.ShapeDtypeStruct((seq, width), BF),
        jax.ShapeDtypeStruct((seq, 128), F32),
        jax.ShapeDtypeStruct((8, width), F32),
    )
    args = (pair, out_w, vec, cot, in_rows, back_rows)
    return run(
        forward_kernel, "forward", 17, (place,), args, (1,),
        [whole(a.shape) for a in args], [whole(x.shape) for x in shapes], shapes, mib=24,
    )


def backward_kernel(last, outer_ref, start_ref, slope_ref, in_ref, back_ref, *refs):
    step = pl.program_id(0)
    if last:
        normal_ref, scale_ref, out_w_ref, vec_ref, two_ref, send_ref, keep_ref, total_ref, branch_ref, att_ref = refs
    else:
        send_ref, keep_ref, total_ref = refs
    grad_inner = (dot_nt(outer_ref[...], back_ref[...]) * slope_ref[...]).astype(BF)
    more = dot_nn(grad_inner, in_ref[...])

    @pl.when(step == 0)
    def _():
        send_ref[...] = grad_inner
        total_ref[...] = start_ref[...] + more

    @pl.when(step > 0)
    def _():
        keep_ref[...] = grad_inner
        total_ref[...] += more

    if last:

        @pl.when(step == pl.num_programs(0) - 1)
        def _():
            grad = total_ref[...]
            normal = normal_ref[...]
            seq = grad.shape[0]
            one = jnp.sum(grad * normal, axis=0, keepdims=True)
            two = jnp.sum(grad, axis=0, keepdims=True)
            lines = [one, two, two_ref[0:2, :], jnp.zeros((12, grad.shape[1]), F32)]
            branch_ref[seq:, :] = jnp.concatenate(lines, axis=0).astype(BF)
            grad_sum = norm_back(grad, normal, scale_ref[:, 0:1], vec_ref[0:1, :])
            total_ref[...] = grad_sum
            branch = grad_sum.astype(BF)
            branch_ref[:seq, :] = branch
            att_ref[...] = dot_nt(branch, out_w_ref[...]).astype(BF)


def backward(outer, start, slope, in_rows, back_rows, high, rest, after):
    seq, width = outer.shape
    units = in_rows.shape[0]
    step = units // 4
    chunk = lambda i: 2 * (1 - i) + high
    shapes = [jax.ShapeDtypeStruct((seq, step), BF)] * 2 + [jax.ShapeDtypeStruct((seq, width), F32)]
    if rest:
        shapes += [jax.ShapeDtypeStruct((seq + 16, width), BF), jax.ShapeDtypeStruct((seq, width), BF)]
    return run(
        functools.partial(backward_kernel, bool(rest)), "backward", 7, (),
        (outer, start, slope, in_rows, back_rows) + tuple(rest), (2,),
        [
            whole((seq, width)),
            whole((seq, width)),
            pl.BlockSpec((seq, step), lambda i: (0, chunk(i))),
            pl.BlockSpec((step, width), lambda i: (chunk(i), 0)),
            pl.BlockSpec((step, width), lambda i: (chunk(i), 0)),
        ]
        + [whole(r.shape) for r in rest],
        [whole(x.shape) for x in shapes],
        shapes,
        (),
        after,
    )


def unit_grad_kernel(own_ref, recv_ref, own_other, recv_other, out_ref):
    out_ref[...] = (dot_tn(own_ref[...], own_other[...]) + dot_tn(recv_ref[...], recv_other[...])).astype(BF)


def unit_grad(own, recv, own_other, recv_other, column, after):
    seq, width = own_other.shape
    step = 768
    shape = jax.ShapeDtypeStruct((step, width), BF)
    piece = pl.BlockSpec((seq, step), lambda i: (0, column))
    (out,), token = run(
        unit_grad_kernel, "unit_grad", 1.5, (), (own, recv, own_other, recv_other), (1,),
        [piece, piece, whole(own_other.shape), whole(recv_other.shape)], [whole(shape.shape)], [shape], (), after,
    )
    return out, token


def hot_columns(place, rows):
    return (iota((rows, place.shape[1]), 0) == place).astype(F32).astype(BF)


def move_kernel(order_ref, own_ref, recv_ref, own_out, recv_out):
    hot = hot_columns(order_ref[0:1, :], own_ref.shape[2])
    own_out[...] = dot_nn(own_ref[0], hot).astype(BF)
    recv_out[...] = dot_nn(recv_ref[0], hot).astype(BF)


def move(order, pair, pair_recv, after):
    _, seq, width = pair.shape
    shape = jax.ShapeDtypeStruct((seq, width), BF)
    part = pl.BlockSpec((1, seq, width), lambda i: (0, 0, 0))
    return run(
        move_kernel, "move", 1.5, (), (order, pair, pair_recv), (1,),
        [whole(order.shape), part, part], [whole(shape.shape)] * 2, [shape] * 2, (), after,
    )


def out_grad_kernel(spots_ref, branch_ref, branch_recv, att_ref, att_recv, low_ref, high_ref):
    seq, width = att_ref.shape[1:]
    rows = low_ref.shape[0]
    hot = hot_columns(spots_ref[0:1, :], width)
    moved = dot_nn(branch_ref[:seq, :], hot).astype(BF)
    moved_recv = dot_nn(branch_recv[:seq, :], hot).astype(BF)
    grad = (dot_tn(moved, att_ref[0]) + dot_tn(moved_recv, att_recv[0])).astype(BF)
    sums = branch_ref[seq:, :].astype(F32) + branch_recv[seq:, :].astype(F32)
    lines = jnp.concatenate([sums, jnp.zeros((112, width), F32)], axis=0).astype(BF)
    sums = jnp.transpose(dot_nn(lines, hot)).astype(BF)
    for i, out in enumerate((low_ref, high_ref)):
        out[:, :width] = grad[i * rows : (i + 1) * rows]
        out[:, width:] = sums[i * rows : (i + 1) * rows]


def out_grad(spots, branch, branch_recv, pair, pair_recv, after):
    _, seq, width = pair.shape
    shape = jax.ShapeDtypeStruct((width // 4, width + 128), BF)
    part = pl.BlockSpec((1, seq, width), lambda i: (1, 0, 0))
    return run(
        out_grad_kernel, "out_grad", 2, (), (spots, branch, branch_recv, pair, pair_recv), (1,),
        [whole(spots.shape), whole(branch.shape), whole(branch.shape), part, part],
        [whole(shape.shape)] * 2, [shape] * 2, (), after,
    )


def side_grad_kernel(moved_ref, moved_recv, gproj_ref, gproj_recv, out_low, out_high, low_ref, high_ref):
    half = moved_ref.shape[1] // 2
    rows = half // 2
    low_ref[:, 6 * half :] = out_low[...]
    high_ref[:, 6 * half :] = out_high[...]
    for c in range(3):
        grad = (dot_tn(moved_ref[...], gproj_ref[c]) + dot_tn(moved_recv[...], gproj_recv[c])).astype(BF)
        for k in range(2):
            at = (3 * k + c) * half
            low_ref[:, at : at + half] = grad[2 * k * rows : (2 * k + 1) * rows]
            high_ref[:, at : at + half] = grad[(2 * k + 1) * rows : (2 * k + 2) * rows]


def side_grad(*args, after):
    half = args[0].shape[1] // 2
    shapes = [jax.ShapeDtypeStruct((half // 2, 8 * half + 128), BF)] * 2
    return run(
        side_grad_kernel, "side_grad", 4, (), args, (1,),
        [whole(a.shape) for a in args], [whole(x.shape) for x in shapes], shapes, (), after,
    )


def swap_head(x):
    return lax.ppermute(x, "head", [(0, 1), (1, 0)])


def swap_dp(x, bit):
    return lax.ppermute(x, "dp", [(i, i ^ bit) for i in range(lax.axis_size("dp"))])


def swap_both(x, bits):
    count = lax.axis_size("dp")
    pairs = [(2 * i + h, 2 * (i ^ bits[h]) + h) for i in range(count) for h in range(2)]
    return lax.ppermute(x, ("dp", "head"), pairs)


def add_kernel(keep_low, keep_high, recv_low, recv_high, send, keep):
    send[...] = keep_high[...] + recv_high[...]
    keep[...] = keep_low[...] + recv_low[...]


def add_whole_kernel(keep_ref, recv_ref, send, keep):
    half = keep.shape[0]
    total = keep_ref[...].astype(F32) + recv_ref[...].astype(F32)
    send[...] = total[half:].astype(BF)
    keep[...] = total[:half].astype(BF)


def add_halves(keep, recv, after=()):
    half, width = recv.shape[0] // 2, recv.shape[1]
    shape = jax.ShapeDtypeStruct((half, width), BF)
    if half % 16 and half % 8 == 0:
        return run(
            add_whole_kernel, "add_halves", 1, (), (keep, recv), (1,), [whole(recv.shape)] * 2,
            [whole(shape.shape)] * 2, [shape] * 2, (), after,
        )
    if half % 16:
        total = keep + recv
        return (total[half:], total[:half]), None
    steps = 2 if half % 32 == 0 and half >= 384 else 1
    block = half // steps
    low = pl.BlockSpec((block, width), lambda i: (i, 0))
    high = pl.BlockSpec((block, width), lambda i: (i + steps, 0))
    return run(
        add_kernel, "add_halves", 1, (), (keep, keep, recv, recv), (steps,), [low, high, low, high],
        [low, low], [shape, shape], (), after,
    )


class Sum:
    def __init__(self, bits, send, low=None):
        self.bits, self.keep, self.done = bits, low, 0
        self.swap(send)

    def swap(self, send):
        k = self.done
        if k < 2:
            self.recv = swap_both(send, (self.bits[0], self.bits[1]) if k == 0 else (self.bits[1], self.bits[0]))
        else:
            self.recv = swap_dp(send, self.bits[k])
        self.done += 1

    def step(self, token):
        (send, self.keep), token_out = add_halves(self.keep, self.recv, (token,))
        self.swap(send)
        return token if token_out is None else token_out

    def result(self):
        return self.keep.astype(F32) + self.recv.astype(F32)


def reversed_bits(count):
    bits = count.bit_length() - 1
    return [sum(((i >> b) & 1) << (bits - 1 - b) for b in range(bits)) for i in range(count)]


def swap_low(i):
    return (i & ~3) | ((i & 1) << 1) | ((i >> 1) & 1)


def body(
    token_ids,
    lengths,
    embed_table,
    qkv_weight,
    out_weight,
    first_gain,
    first_bias,
    in_weight,
    back_weight,
    second_gain,
    term_vector,
    cotangent,
):
    dp = lax.axis_index("dp")
    head = lax.axis_index("head")
    owners = lax.axis_size("dp")
    bits = [1 << b for b in range(owners.bit_length() - 1)]
    device = dp * 2 + head
    seq = token_ids.shape[0]
    table_rows, half = embed_table.shape
    width = 2 * half
    units = back_weight.shape[0]
    cap = 4 * seq // owners
    slots = owners * cap

    ids = jnp.broadcast_to(token_ids.reshape(1, seq), (2 * owners, seq))
    ids = lax.all_to_all(ids, ("dp", "head"), split_axis=0, concat_axis=0, tiled=True)
    picked, asked, slot_row, slot_col = pick(jnp.stack([dp, head]), ids, embed_table, cap)
    got = lax.all_to_all(picked.reshape(owners, cap, half), "dp", split_axis=0, concat_axis=0, tiled=True)

    rev = reversed_bits(owners)
    ways = jnp.array([rev, [swap_low(r) for r in rev]], jnp.int32)
    keep_blocks, send_blocks = (ways[head] ^ dp) * 2 + head, (ways[1 - head] ^ dp) * 2 + 1 - head
    unit_order = jnp.concatenate([keep_blocks, send_blocks])
    back_rows = jnp.take(back_weight.reshape(2 * owners, -1, width), unit_order, axis=0, mode="clip").reshape(units, width)
    in_rows = jnp.take(in_weight.T.reshape(2 * owners, -1, width), unit_order, axis=0, mode="clip").reshape(units, width)
    weight = jnp.concatenate([qkv_weight, swap_head(qkv_weight)], axis=2)
    out_block = width // (2 * owners)
    inside = jnp.arange(out_block, dtype=jnp.int32)[None, :]
    lines = lambda start: (start[:, None] * out_block + inside).reshape(1, half)
    spots = lines(keep_blocks)
    order = jnp.concatenate([lines(keep_blocks - head), lines(keep_blocks - head + 1)], axis=1)
    vec = jnp.concatenate(
        [jnp.stack([first_gain, first_bias, second_gain, term_vector]), jnp.zeros((4, width), F32)], axis=0
    )
    asked_rows = asked[:owners].reshape(slots // 512, 512)
    cot = jnp.broadcast_to(cotangent.reshape(seq, 1), (seq, 128))
    place = jnp.stack([head, lengths[0]]).astype(jnp.int32)

    corner = in_rows[:8, :128] + back_rows[:8, :128] + weight[0, :8, :128]
    send, t = regather(slot_col, got.reshape(slots, half), 1, (corner, vec, cot, spots, order, asked_rows))
    own, _ = regather(slot_col, got.reshape(slots, half), 0, (t,))
    other = swap_head(send)
    (pair, proj, stat), _ = attend(place, own, other, weight)
    pair_recv = swap_head(pair)
    (low, normal, scale, active_send, active, slope, mixed, outer, weights, sums), t = forward(
        place, pair, out_weight, vec, cot, in_rows, back_rows
    )
    low_recv, outer_recv, active_recv = swap_head(low), swap_head(outer), swap_head(active_send)
    (inner_send, inner_high, total), t = backward(outer, mixed, slope, in_rows, back_rows, 1, (), (t,))
    inner_recv = swap_head(inner_send)
    high, t = unit_grad(active, active_recv, outer, outer_recv, 1, (t,))
    back = Sum(bits, high)
    high, t = unit_grad(inner_high, inner_recv, low, low_recv, 0, (t,))
    ins = Sum(bits, high)
    (moved, moved_recv), t = move(order, pair, pair_recv, (t,))
    (inner_send, inner_low, grad_sum, branch, grad_att), t = backward(
        outer, total, slope, in_rows, back_rows, 0, (normal, scale, out_weight, vec, sums), (t,)
    )
    inner_recv, branch_recv = swap_head(inner_send), swap_head(branch)
    (gproj_send, total), t = attend_back(place, proj, grad_att, stat, weight, grad_sum, False, (t,))
    gproj_recv = swap_head(gproj_send)
    back.keep, t = unit_grad(active, active_recv, outer, outer_recv, 0, (t,))
    t = back.step(t)
    ins.keep, t = unit_grad(inner_low, inner_recv, low, low_recv, 0, (t,))
    out_parts, t = out_grad(spots, branch, branch_recv, pair, pair_recv, (t,))
    (gproj, grad_own, grad_send), t = attend_back(place, proj, grad_att, stat, weight, total, True, (t,))
    grad_other = swap_head(grad_send)
    t = back.step(t)
    t = ins.step(t)
    (side_low, side_high), t = side_grad(moved, moved_recv, gproj, gproj_recv, *out_parts, after=(t,))
    side = Sum(bits, side_high, side_low)
    t = back.step(t)
    t = ins.step(t)
    (sent,), t = spread(slot_row, grad_own, grad_other, slots, (t,))
    arrived = lax.all_to_all(sent.reshape(owners, cap, half), "dp", split_axis=0, concat_axis=0, tiled=True)
    t = ins.step(t)
    t = side.step(t)
    t = side.step(t)
    (grad_table,), t = table_grad(asked_rows, arrived.reshape(slots, half), table_rows, (t,))
    while min(back.done, ins.done, side.done) < len(bits):
        for one in (side, ins, back):
            if one.done < len(bits):
                t = one.step(t)
    grad_back, grad_in, side = back.result(), ins.result(), side.result()
    grad_out, vectors = side[:, 6 * half : 8 * half], side[:, 8 * half :]
    grad_qkv = jnp.concatenate([side[:, : 3 * half], side[:, 3 * half : 6 * half]], axis=0)
    grad_qkv = grad_qkv.reshape(-1, 3, half).transpose(1, 0, 2)
    return (
        weights[:, 0],
        grad_table,
        grad_qkv,
        grad_out.T,
        grad_in.T,
        grad_back,
        vectors[:, 0],
        vectors[:, 1],
        vectors[:, 2],
        vectors[:, 3],
    )


def solution(mesh):
    in_specs = (
        P(("dp", "head")),
        P(("dp", "head")),
        P("dp", "head"),
        P(None, None, "head"),
        P(),
        P(),
        P(),
        P(),
        P(),
        P(),
        P(),
        P(("dp", "head")),
    )
    out_specs = (
        P(("dp", "head")),
        P("dp", "head"),
        P(None, "dp", "head"),
        P(None, ("dp", "head")),
        P(None, ("dp", "head")),
        P(("dp", "head"), None),
        P(("dp", "head")),
        P(("dp", "head")),
        P(("dp", "head")),
        P(("dp", "head")),
    )
    return jax.shard_map(body, mesh=mesh, in_specs=in_specs, out_specs=out_specs, check_vma=False)
```
